256 devices in a mesh: cond: 8 (over y, x_hi), space: 32 (over x_lo, z, core).
Axes of the slice: x: 4 (x_hi: 2, x_lo: 2; x = x_hi * 2 + x_lo), y: 4, z: 8, core: 2. Of those that a mesh axis runs over, the one named last changes fastest.
Arguments:
- flow: float32 [16, 3, 512, 2048], P('cond', None, 'space'), may hold values from -4 to 4
- forcing: float32 [16, 2, 512, 2048], P('cond', None, 'space'), may hold values from -4 to 4
- wet: int32 [16, 512, 2048], P('cond', 'space'), may hold values 0 or 1
- depth: float32 [512, 2048], P('space'), may hold values from 0.5 to 2
- limiter: int32 [512, 2048], P('space'), may hold values 0 or 1
- weights: int32 [16], replicated, may hold values from 1 to 9
- bed: float32 [512, 2048], P('space'), may hold values from -6 to 6
- diffusivity: float32 [512, 2048], P('space'), may hold values from 0.2 to 5
Outputs:
- surface: float32 [16, 512, 2048], P('cond', 'space')
- bed_new: float32 [512, 2048], P('space')
The draws below stay inside these ranges and needn't reach their ends.
All inputs are finite; a program needn't handle non-finite values. No bound on the sum of `wet` or of `limiter` on one device may be relied on, other than what follows from the above.
Results may differ from the reference program's by a relative error of at most 0.0001.
Values sent between devices are 32-bit elements; how exact they have to be, the bound alone decides.
A program may use at most 64 MiB of HBM per device.

```python
import math
import jax
import jax.numpy as jnp
from jax import lax

NY = 2048
STEPS = 4
ITERS = 2
NX = 512
CONDS = 16


def set_ends(drawn, stream_key, smallest, high):
    extent = drawn.shape
    place = [jax.random.randint(jax.random.fold_in(stream_key, axis), (), 0, extent[axis]) for axis in range(len(extent))]
    drawn = drawn.at[tuple(place)].set(smallest)
    longest = extent.index(max(extent))
    place[longest] = (place[longest] + 1) % extent[longest]
    return drawn.at[tuple(place)].set(high)


def block_scale(stream_key, shape, pieces, smallest, largest):
    level, own = 1.0, jax.random.fold_in(stream_key, 6)
    for axis_at, blocks in pieces:
        draws = jnp.exp(jax.random.uniform(jax.random.fold_in(own, axis_at), (blocks,), jnp.float32, smallest / len(pieces), largest / len(pieces)))
        level = level * jnp.repeat(draws, shape[axis_at] // blocks).reshape([-1 if axis == axis_at else 1 for axis in range(len(shape))])
    return level


def gaussian(stream_key, shape, scale, reach, pieces=(), dtype=jnp.bfloat16):
    values = scale * jax.random.normal(stream_key, shape, jnp.float32)
    if pieces:
        values = values * block_scale(stream_key, shape, pieces, -0.22, 0.18)
    return jnp.clip(values, -reach, reach).astype(dtype)


def setup_inputs(seed: int = 0) -> dict:
    streams_of = jax.random.split(jax.random.key(seed), 9)
    flow = gaussian(streams_of[0], (CONDS, 3, NX, NY), 0.5, 4.0, ((0, 8), (2, 32)), jnp.float32)
    forcing = gaussian(streams_of[1], (CONDS, 2, NX, NY), 0.5, 4.0, ((0, 8), (2, 32)), jnp.float32)
    wet = set_ends((jax.random.randint(streams_of[2], (CONDS, NX, NY), 0, 8) < 7).astype(jnp.int32), jax.random.fold_in(streams_of[2], 1), 0, 1)
    depth = jnp.clip(jnp.exp(math.log(2.0) - 1.3862944 * jax.random.uniform(streams_of[3], (NX, NY), jnp.float32) ** block_scale(streams_of[3], (NX, NY), ((0, 32),), -0.2, 0.2)), 0.5, 2.0)
    limiter = set_ends((jax.random.randint(streams_of[4], (NX, NY), 0, 2) < 1).astype(jnp.int32), jax.random.fold_in(streams_of[4], 1), 0, 1)
    weights = set_ends(jax.random.randint(streams_of[5], (CONDS,), 1, 10), jax.random.fold_in(streams_of[5], 1), 1, 9).astype(jnp.int32)
    bed = gaussian(streams_of[6], (NX, NY), 1.0, 6.0, ((0, 32),), jnp.float32)
    diffusivity = jnp.clip(jnp.exp(math.log(5.0) - 3.218876 * jax.random.uniform(streams_of[7], (NX, NY), jnp.float32) ** block_scale(streams_of[7], (NX, NY), ((0, 32),), -0.2, 0.2)), 0.2, 5.0)
    return dict(flow=flow, forcing=forcing, wet=wet, depth=depth, limiter=limiter, weights=weights, bed=bed, diffusivity=diffusivity)


time_step = 0.4
gravity = 1.0
friction = 0.1
transport_base = 0.5
morph_factor = 1.0
slope_coeff = 1.0


def row_diff(field):
    padded = jnp.pad(field, ((1, 1), (0, 0)))
    return 0.5 * (padded[2:] - padded[:-2])


def column_diff(field):
    padded = jnp.pad(field, ((0, 0), (1, 1)))
    return 0.5 * (padded[:, 2:] - padded[:, :-2])


def tendency(state_now, depth, wet_mask, force):
    elevation, vel_first, vel_second = state_now[0], state_now[1], state_now[2]
    rate_elev = -(row_diff(depth * vel_first) + column_diff(depth * vel_second))
    rate_first = -gravity * row_diff(elevation) - friction * vel_first + force[0]
    rate_second = -gravity * column_diff(elevation) - friction * vel_second + force[1]
    return wet_mask * jnp.stack([rate_elev, rate_first, rate_second])


def transport(state_now, limit_mask):
    vel_first, vel_second = state_now[1], state_now[2]
    energy = vel_first * vel_first + vel_second * vel_second
    factor = (transport_base + energy) / (1.0 + limit_mask * energy)
    return vel_first * factor, vel_second * factor


def neighbours(padded):
    return [padded[:-2, 1:-1], padded[2:, 1:-1], padded[1:-1, :-2], padded[1:-1, 2:]]


def apply_op(field, coefs):
    near = neighbours(jnp.pad(field, 1))
    total = coefs[0] * (field - near[0]) + coefs[1] * (field - near[1])
    total = total + coefs[2] * (field - near[2]) + coefs[3] * (field - near[3])
    return field + slope_coeff * total


def reference(flow, forcing, wet, depth, limiter, weights, bed, diffusivity):
    limit_mask = limiter.astype(jnp.float32)

    def one_condition(items):
        state_now, force, wet_int = items
        wet_mask = wet_int.astype(jnp.float32)[None]
        bed_change = jnp.zeros(state_now.shape[1:], jnp.float32)
        for stepper in range(STEPS):
            first_section = state_now + time_step * tendency(state_now, depth, wet_mask, force)
            state_now = 0.5 * (state_now + first_section + time_step * tendency(first_section, depth, wet_mask, force))
            flux_first, flux_second = transport(state_now, limit_mask)
            bed_change = bed_change - morph_factor * (row_diff(flux_first) + column_diff(flux_second))
        return state_now[0], bed_change

    surface, changes = lax.map(one_condition, (flow, forcing, wet))
    weight_all = weights.astype(jnp.float32)
    increment = jnp.sum(weight_all[:, None, None] * changes, 0) / jnp.sum(weight_all)
    padded = jnp.pad(diffusivity, 1)
    centre = padded[1:-1, 1:-1]
    coefs = [centre * other / (centre + other) for other in neighbours(padded)]
    rhs = bed + increment
    solution = jnp.zeros_like(rhs)
    residual = rhs
    direction = rhs
    norm_now = jnp.sum(rhs * rhs)
    for sweep in range(ITERS):
        image = apply_op(direction, coefs)
        alpha = norm_now / jnp.sum(direction * image)
        solution = solution + alpha * direction
        if sweep + 1 < ITERS:
            residual = residual - alpha * image
            norm_next = jnp.sum(residual * residual)
            direction = residual + (norm_next / norm_now) * direction
            norm_now = norm_next
    return surface, solution
```

```python
import functools

import jax
import jax.numpy as jnp
from jax import lax
from jax.experimental import pallas as pl
from jax.experimental.pallas import tpu as pltpu
from jax.sharding import PartitionSpec as P

MESH = pl.DeviceIdType.MESH
F32 = jnp.float32

STEPS = 4
TIME_STEP = 0.4
GRAVITY = 1.0
FRICTION = 0.1
TRANSPORT_BASE = 0.5
MORPH_FACTOR = 1.0
SLOPE_COEFF = 1.0

LANES = 128
ROWS = 16
HALO = 8
TALL = ROWS + 2 * HALO
HALF_STEPS = 2 * STEPS
EDGE = 18
UNROLL = 4


def kernel(
    nc,
    ns,
    flow,
    forcing,
    wet,
    depth,
    limiter,
    weights,
    bed,
    diffusivity,
    surface,
    bed_new,
    flow_own,
    force_own,
    wet_own,
    grid_own,
    lim_own,
    w_own,
    flow_rim,
    force_rim,
    wet_rim,
    grid_rim,
    eta,
    vel_a,
    vel_b,
    dva,
    dvb,
    mask,
    fa,
    fb,
    dep,
    lim,
    qa,
    qb,
    part,
    landing,
    whole,
    from_up,
    from_dn,
    diff,
    kd,
    kr,
    kl,
    b,
    y,
    sums,
    surf,
    result,
    load_sem,
    store_sem,
    rim_send,
    rim_recv,
    rs_send,
    rs_recv,
    ag_send,
    ag_recv,
    up_recv,
    dn_recv,
    sum_send,
    sum_recv,
    known,
):
    c = lax.axis_index("cond")
    s = lax.axis_index("space")
    blocks = kd.shape[0] - 2
    conds = flow.shape[0]
    share = blocks // nc
    lane = lax.broadcasted_iota(jnp.int32, (8, LANES), 1)
    sub = lax.broadcasted_iota(jnp.int32, (8, LANES), 0)

    def wide(pattern, n):
        return pattern if n == 1 else jnp.concatenate([pattern] * n, 0)

    def each_block(body):
        def group(g, carry):
            for r in range(UNROLL):
                body(g * UNROLL + r + 1)
            return carry

        lax.fori_loop(0, blocks // UNROLL, group, 0)

    loads = []

    def load(src, dst):
        copy = pltpu.make_async_copy(src, dst, load_sem.at[len(loads)])
        copy.start()
        loads.append(copy)
        return copy

    l_depth = load(depth, grid_own.at[0])
    l_cond = []
    for j in range(conds):
        l_cond.append(
            [
                load(flow.at[j], flow_own.at[j]),
                load(forcing.at[j], force_own.at[j]),
                load(wet.at[j], wet_own.at[j]),
            ]
        )
    l_w = load(weights, w_own)
    l_lim = load(limiter, lim_own)
    l_diff = load(diffusivity, grid_own.at[1])
    l_bed = load(bed, grid_own.at[2])

    near_space = [(c, lax.rem(s + d, ns)) for d in (1, ns - 1)]
    near_cond = [(c + 1 - 2 * lax.rem(c, 2), s)]
    near_cond += [(lax.rem(c + d, nc), s) for d in (2, nc - 2)]
    near = near_space + near_cond
    barrier = pltpu.get_barrier_semaphore()
    for peer in near:
        pl.semaphore_signal(barrier, inc=1, device_id=peer, device_id_type=MESH)

    for ref in (eta, dvb):
        for block in (0, blocks + 1):
            ref[:, block] = jnp.zeros((conds * HALF_STEPS, TALL, LANES), F32)
    for ref in (qb, diff, b, y):
        for block in (0, blocks + 1):
            ref[block] = jnp.zeros(ref.shape[1:], F32)
    whole[:, 16:24, :] = jnp.zeros((blocks, 8, LANES), F32)
    from_up[...] = jnp.zeros(from_up.shape, F32)
    from_dn[...] = jnp.zeros(from_dn.shape, F32)
    qa[...] = jnp.zeros(qa.shape, F32)
    for block in range(1, blocks + 1):
        qb[block] = jnp.zeros((TALL, LANES), F32)
        y[block] = jnp.zeros((TALL, LANES), F32)
    pl.semaphore_wait(barrier, len(near))

    slow = lax.rem(s, 2)
    fast = 1 - slow

    def has(side):
        return jnp.where(side == 0, s > 0, s < ns - 1)

    def rim_copies(side, slot_side):
        peer = (c, s - 1 + 2 * side)
        rows = pl.ds(pl.multiple_of(HALO * side, HALO), HALO)
        pairs = [(depth.at[rows], grid_rim.at[slot_side, 0])]
        for j in range(conds):
            pairs.append((flow.at[j, :, rows], flow_rim.at[slot_side, j]))
            pairs.append((forcing.at[j, :, rows], force_rim.at[slot_side, j]))
            pairs.append((wet.at[j, rows], wet_rim.at[slot_side, j]))
            if j == 0:
                pairs.append((diffusivity.at[rows], grid_rim.at[slot_side, 1]))
                pairs.append((bed.at[rows], grid_rim.at[slot_side, 2]))
        def copy(i):
            src, dst = pairs[i]
            return pltpu.make_async_remote_copy(
                src,
                dst,
                rim_send.at[side, i],
                rim_recv.at[slot_side, i],
                device_id=peer,
                device_id_type=MESH,
            )

        return [functools.partial(copy, i) for i in range(len(pairs))]

    def start_rims(side):
        for copy in rim_copies(side, 1 - side):
            copy().start()

    def wait_rims(side, which):
        copies = rim_copies(side, side)
        for i in which:
            copies[i]().wait_recv()

    pl.when(has(slow))(lambda: start_rims(slow))
    start_rims(fast)

    def tell(step, peers):
        for peer in peers:
            pl.semaphore_signal(
                known.at[step], inc=1, device_id=peer, device_id_type=MESH
            )
        return len(peers)

    def ring(d):
        return [(c, lax.rem(s + d, ns)), (c, lax.rem(s + ns - d, ns))]

    n0 = tell(0, near)

    def fill_grid(src, dst, rows, real=None):
        def body(k):
            at = pl.ds(pl.multiple_of((k - 1) * LANES, LANES), LANES)
            value = src[:, at]
            if real is not None:
                value = jnp.where(real, value, jnp.zeros_like(value))
            dst[k, rows, :] = value

        each_block(body)

    def fill_cond(j, flow_src, force_src, wet_src, rows, real=None):
        at0 = j * HALF_STEPS

        def body(k):
            at = pl.ds(pl.multiple_of((k - 1) * LANES, LANES), LANES)

            def get(value):
                if real is None:
                    return value
                return jnp.where(real, value, jnp.zeros_like(value))

            d = dep[k, rows, :]
            e = get(flow_src[0, :, at])
            u = get(flow_src[1, :, at])
            v = get(flow_src[2, :, at])
            m = get(wet_src[:, at]).astype(F32) * (0.5 * TIME_STEP)
            eta[at0, k, rows, :] = e
            vel_a[at0, k, rows, :] = u
            vel_b[at0, k, rows, :] = v
            dva[at0, k, rows, :] = d * u
            dvb[at0, k, rows, :] = d * v
            mask[j, k, rows, :] = m
            fa[j, k, rows, :] = 2.0 * m * get(force_src[0, :, at])
            fb[j, k, rows, :] = 2.0 * m * get(force_src[1, :, at])

        each_block(body)

    own = pl.ds(HALO, ROWS)
    l_depth.wait()
    fill_grid(grid_own.at[0], dep, own)

    def advance(j, t, k, start, n):
        at = j * HALF_STEPS + t
        first_lane, last_lane = wide(lane, n) == 0, wide(lane, n) == LANES - 1
        rows, up, dn = (pl.ds(start + d, 8 * n) for d in (0, -1, 1))

        def across(ref):
            here = ref[at, k, rows, :]
            right = jnp.where(first_lane, ref[at, k + 1, rows, :], here)
            left = jnp.where(last_lane, ref[at, k - 1, rows, :], here)
            return here, pltpu.roll(right, LANES - 1, 1) - pltpu.roll(left, 1, 1)

        e, e_across = across(eta)
        _, h_across = across(dvb)
        m = mask[j, k, rows, :]
        keep = 1.0 - (2.0 * FRICTION) * m
        e_next = e - m * (dva[at, k, dn, :] - dva[at, k, up, :] + h_across)
        slope = GRAVITY * m
        u_next = keep * vel_a[at, k, rows, :] + fa[j, k, rows, :]
        u_next = u_next - slope * (eta[at, k, dn, :] - eta[at, k, up, :])
        v_next = keep * vel_b[at, k, rows, :] + fb[j, k, rows, :] - slope * e_across
        return e_next, u_next, v_next

    def put(j, t, k, start, n, state):
        at = j * HALF_STEPS + t
        rows = pl.ds(start, 8 * n)
        e, u, v = state
        d = dep[k, rows, :]
        eta[at, k, rows, :] = e
        vel_a[at, k, rows, :] = u
        vel_b[at, k, rows, :] = v
        dva[at, k, rows, :] = d * u
        dvb[at, k, rows, :] = d * v

    def first(j, t, start, n):
        each_block(lambda k: put(j, t, k, start, n, advance(j, t - 1, k, start, n)))

    def second(j, t, start, n, weight, valid=None, last=None):
        def body(k):
            at = j * HALF_STEPS + t - 2
            rows = pl.ds(start, 8 * n)
            e, u, v = advance(j, t - 1, k, start, n)
            e = 0.5 * (eta[at, k, rows, :] + e)
            u = 0.5 * (vel_a[at, k, rows, :] + u)
            v = 0.5 * (vel_b[at, k, rows, :] + v)
            if last is None:
                put(j, t, k, start, n, (e, u, v))
            else:
                cols = pl.ds(pl.multiple_of((k - 1) * LANES, LANES), LANES)
                surf[j, last, cols] = e
            energy = u * u + v * v
            factor = weight * (TRANSPORT_BASE + energy)
            factor = factor / (1.0 + lim[k, rows, :] * energy)
            add_a, add_b = u * factor, v * factor
            if valid is not None:
                add_a = jnp.where(valid, add_a, 0.0)
                add_b = jnp.where(valid, add_b, 0.0)
            qa[k, rows, :] = qa[k, rows, :] + add_a
            qb[k, rows, :] = qb[k, rows, :] + add_b

        each_block(body)

    def interior(j, weight):
        for t in range(1, HALF_STEPS):
            count = ROWS - 2 * t
            n = -(-count // 8)
            if t % 2:
                first(j, t, HALO + t, n)
            else:
                valid = None
                if count % 8:
                    place = jnp.concatenate([sub + 8 * i for i in range(n)], 0)
                    valid = place < count
                second(j, t, HALO + t, n, weight, valid)

    def side_steps(j, side, weight):
        def pair(p, carry):
            t = 2 * p + 1
            first(j, t, jnp.where(side == 0, t, 24 - t), 1)
            t = 2 * p + 2
            second(j, t, jnp.where(side == 0, t, 24 - t), 1, weight)
            return carry

        lax.fori_loop(0, STEPS - 1, pair, 0)
        t = HALF_STEPS - 1
        first(j, t, jnp.where(side == 0, t, 24 - t), 1)
        rows = pl.ds(pl.multiple_of(8 * side, 8), 8)
        second(j, t + 1, pl.multiple_of(8 + 8 * side, 8), 1, weight, last=rows)

    l_w.wait()
    weight = [w_own[0, conds * c + j].astype(F32) for j in range(conds)]
    w_sum = w_own[0, 0]
    for i in range(1, nc * conds):
        w_sum = w_sum + w_own[0, i]
    w_sum = w_sum.astype(F32)

    def lim_rows():
        l_lim.wait()

        def body(k):
            at = pl.ds(pl.multiple_of((k - 1) * LANES, LANES), LANES)
            lim[k, own, :] = lim_own[:, at].astype(F32)
            lim[k, 0:8, :] = jnp.zeros((8, LANES), F32)
            lim[k, 24:32, :] = jnp.zeros((8, LANES), F32)

        each_block(body)

    lim_rows()
    for j in range(conds):
        for copy in l_cond[j]:
            copy.wait()
        fill_cond(j, flow_own.at[j], force_own.at[j], wet_own.at[j], own)
        interior(j, weight[j])

    pl.semaphore_wait(known.at[0], n0)
    n1 = tell(1, near + ring(2))
    l_diff.wait()
    l_bed.wait()
    fill_grid(grid_own.at[1], diff, own)
    fill_grid(grid_own.at[2], b, own)

    def rim_rows(side):
        return pl.ds(pl.multiple_of(24 * side, 8), 8)

    def side_grid(side):
        fill_grid(grid_rim.at[side, 0], dep, rim_rows(side), has(side))

    def side_cond(side, j):
        fill_cond(
            j,
            flow_rim.at[side, j],
            force_rim.at[side, j],
            wet_rim.at[side, j],
            rim_rows(side),
            has(side),
        )
        side_steps(j, side, weight[j])

    for j in range(conds):
        if j == 0:
            wait_rims(fast, (0, 1, 2, 3))
            side_grid(fast)
        else:
            at = 3 + 3 * j
            wait_rims(fast, range(at, at + 3))
        side_cond(fast, j)
    wait_rims(fast, (4, 5))
    fill_grid(grid_rim.at[fast, 1], diff, rim_rows(fast))
    fill_grid(grid_rim.at[fast, 2], b, rim_rows(fast))

    pl.semaphore_wait(known.at[1], n1)
    n2 = tell(2, near + ring(4))

    pl.when(has(slow))(lambda: wait_rims(slow, (0, 1, 2, 3)))
    side_grid(slow)
    side_cond(slow, 0)
    pl.when(has(slow))(lambda: wait_rims(slow, (4, 5)))
    fill_grid(grid_rim.at[slow, 1], diff, rim_rows(slow), has(slow))
    fill_grid(grid_rim.at[slow, 2], b, rim_rows(slow), has(slow))

    first_lane3 = wide(lane, 3) == 0
    last_lane3 = wide(lane, 3) == LANES - 1

    def faces(k):
        rows, dn = pl.ds(7, 24), pl.ds(8, 24)

        def face(p, q):
            total = p + q
            return SLOPE_COEFF * p * q / jnp.where(total > 0.0, total, 1.0)

        d = diff[k, rows, :]
        right = jnp.where(first_lane3, diff[k + 1, rows, :], d)
        left = jnp.where(last_lane3, diff[k - 1, rows, :], d)
        kd[k, rows, :] = face(d, diff[k, dn, :])
        kr[k, rows, :] = face(d, pltpu.roll(right, LANES - 1, 1))
        kl[k, rows, :] = face(d, pltpu.roll(left, 1, 1))

    each_block(faces)
    pl.semaphore_wait(known.at[2], n2)
    n3 = tell(3, ring(8))

    for j in range(1, conds):
        at = 3 + 3 * j
        pl.when(has(slow))(lambda at=at: wait_rims(slow, range(at, at + 3)))
        side_cond(slow, j)

    out_surf = pltpu.make_async_copy(surf, surface, store_sem.at[0])
    out_surf.start()

    scale = (-0.5 * MORPH_FACTOR) / w_sum

    def clear_rims(k):
        for ref in (qa, qb):
            ref[k, 0:8, :] = jnp.zeros((8, LANES), F32)
            ref[k, 24:32, :] = jnp.zeros((8, LANES), F32)

    each_block(clear_rims)

    def divergence(k):
        rows, up, dn = pl.ds(7, 24), pl.ds(6, 24), pl.ds(8, 24)
        here = qb[k, rows, :]
        right = jnp.where(first_lane3, qb[k + 1, rows, :], here)
        left = jnp.where(last_lane3, qb[k - 1, rows, :], here)
        total = pltpu.roll(right, LANES - 1, 1) - pltpu.roll(left, 1, 1)
        total = total + (qa[k, dn, :] - qa[k, up, :])
        part[k - 1] = scale * total

    each_block(divergence)

    def remote(src, dst, send, recv, peer):
        copy = pltpu.make_async_remote_copy(
            src, dst, send, recv, device_id=peer, device_id_type=MESH
        )
        copy.start()

    for d in range(1, nc):
        peer = lax.rem(c + d, nc)
        remote(
            part.at[pl.ds(peer * share, share), 0:EDGE],
            landing.at[d, :, 0:EDGE],
            rs_send,
            rs_recv,
            (peer, s),
        )
    mine = pl.ds(c * share, share)
    landed = landing.at[1:nc, :, 0:EDGE]
    pltpu.make_async_copy(landed, landed, rs_recv).wait()
    total = part[mine]
    for d in range(1, nc):
        total = total + landing[d]
    whole[mine, 0:16, :] = total[:, 0:16]
    whole[mine, 16:EDGE, :] = total[:, 16:EDGE]

    for d in range(1, nc):
        peer = lax.rem(c + d, nc)
        block = whole.at[mine, 0:EDGE]
        remote(block, block, ag_send.at[0], ag_recv, (peer, s))

    def edges(side):
        rows = slice(0, 3) if side == 0 else slice(EDGE - 3, EDGE)
        land, recv = (from_dn, dn_recv) if side == 0 else (from_up, up_recv)
        for d in range(nc):
            peer = lax.rem(c + d, nc)
            remote(
                whole.at[mine, rows],
                land.at[mine, 0:3],
                ag_send.at[1 + side],
                recv,
                (peer, s - 1 + 2 * side),
            )

    pl.when(s > 0)(lambda: edges(0))
    pl.when(s < ns - 1)(lambda: edges(1))
    pltpu.make_async_copy(landed, landed, ag_recv).wait()
    edge_up, edge_dn = from_up.at[:, 0:3], from_dn.at[:, 0:3]

    def wait_up():
        pltpu.make_async_copy(edge_up, edge_up, up_recv).wait()

    def wait_dn():
        pltpu.make_async_copy(edge_dn, edge_dn, dn_recv).wait()

    pl.when(s > 0)(wait_up)
    pl.when(s < ns - 1)(wait_dn)

    def assemble(k):
        rows = pl.ds(7, 24)
        b[k, rows, :] = b[k, rows, :] + whole[k - 1]
        rows = pl.ds(6, 8)
        b[k, rows, :] = b[k, rows, :] + from_up[k - 1]
        rows = pl.ds(23, 8)
        b[k, rows, :] = b[k, rows, :] + from_dn[k - 1]

    each_block(assemble)

    def fold(value):
        return value[0:8] + value[8:16]

    def first_moments(g, carry):
        bb, bl, ll = carry
        for r in range(UNROLL):
            k = g * UNROLL + r + 1
            rows, up, dn = pl.ds(8, 24), pl.ds(7, 24), pl.ds(9, 24)
            here = b[k, pl.ds(8, 24), :]
            right = jnp.where(first_lane3, b[k + 1, rows, :], here)
            left = jnp.where(last_lane3, b[k - 1, rows, :], here)
            to_dn = here - b[k, pl.ds(9, 24), :]
            to_up = here - b[k, up, :]
            to_right = here - pltpu.roll(right, LANES - 1, 1)
            to_left = here - pltpu.roll(left, 1, 1)
            f_dn = kd[k, rows, :] * to_dn
            f_right = kr[k, rows, :] * to_right
            image = f_dn + kd[k, up, :] * to_up + f_right + kl[k, rows, :] * to_left
            y[k, rows, :] = image
            bb = bb + fold(here * here)
            bl = bl + fold(f_dn * to_dn + f_right * to_right)
            ll = ll + fold(image * image)
        return bb, bl, ll

    zero = jnp.zeros((8, LANES), F32)
    bb, bl, ll = lax.fori_loop(0, blocks // UNROLL, first_moments, (zero, zero, zero))

    first_lane2 = wide(lane, 2) == 0

    def last_moment(g, carry):
        for r in range(UNROLL):
            k = g * UNROLL + r + 1
            here = y[k, own, :]
            right = jnp.where(first_lane2, y[k + 1, own, :], here)
            to_dn = here - y[k, pl.ds(HALO + 1, ROWS), :]
            to_right = here - pltpu.roll(right, LANES - 1, 1)
            energy = kd[k, own, :] * to_dn * to_dn + kr[k, own, :] * to_right * to_right
            carry = carry + fold(energy)
        return carry

    lyl = lax.fori_loop(0, blocks // UNROLL, last_moment, zero)

    tile = zero
    for i, value in enumerate((bb, bl, ll, lyl)):
        tile = jnp.where(sub == i, jnp.sum(value, 0, keepdims=True), tile)
    sums[0] = tile
    pl.semaphore_wait(known.at[3], n3)
    for d in range(1, ns):
        remote(
            sums.at[0], sums.at[d], sum_send, sum_recv, (c, lax.rem(s + d, ns))
        )
    others = sums.at[1:ns]
    pltpu.make_async_copy(others, others, sum_recv).wait()
    total = jnp.sum(jnp.sum(sums[...], 0), 1, keepdims=True)
    s_bb, s_bl, s_ll, s_lyl = (total[i : i + 1] for i in range(4))
    m1, m2, m3 = s_bl / s_bb, s_ll / s_bb, s_lyl / s_bb
    alpha0 = 1.0 / (1.0 + m1)
    beta = (m2 - m1 * m1) * alpha0 * alpha0
    p_b = m1 * alpha0 + beta
    p_l = alpha0
    pp = p_b * p_b - 2.0 * p_b * p_l * m1 + p_l * p_l * m2
    plp = p_b * p_b * m1 - 2.0 * p_b * p_l * m2 + p_l * p_l * m3
    alpha1 = beta / (pp + plp)
    x_b = alpha0 + alpha1 * p_b
    x_l = -alpha1 * p_l

    def finish(k):
        at = pl.ds(pl.multiple_of((k - 1) * LANES, LANES), LANES)
        result[:, at] = x_b * b[k, own, :] + x_l * y[k, own, :]

    each_block(finish)
    out_bed = pltpu.make_async_copy(result, bed_new, store_sem.at[1])
    out_bed.start()

    def sent(side):
        for copy in rim_copies(side, 1 - side):
            copy().wait_send()

    pl.when(has(slow))(lambda: sent(slow))
    sent(fast)
    pltpu.make_async_copy(landed, landed, rs_send).wait()
    pltpu.make_async_copy(landed, landed, ag_send.at[0]).wait()

    def sent_up():
        pltpu.make_async_copy(edge_dn, edge_dn, ag_send.at[1]).wait()

    def sent_dn():
        pltpu.make_async_copy(edge_up, edge_up, ag_send.at[2]).wait()

    pl.when(s > 0)(sent_up)
    pl.when(s < ns - 1)(sent_dn)
    pltpu.make_async_copy(others, others, sum_send).wait()
    out_surf.wait()
    out_bed.wait()


def local(nc, ns, flow, forcing, wet, depth, limiter, weights, bed, diffusivity):
    conds, ny = flow.shape[0], flow.shape[-1]
    blocks = ny // LANES
    dma = pltpu.SemaphoreType.DMA

    def vmem(*shape, dtype=F32):
        return pltpu.VMEM(shape, dtype)

    def state():
        return vmem(conds * HALF_STEPS, blocks + 2, TALL, LANES)

    def per_cond():
        return vmem(conds, blocks + 2, TALL, LANES)

    def grid():
        return vmem(blocks + 2, TALL, LANES)

    rims = 3 + 3 * conds
    any_space = pl.BlockSpec(memory_space=pl.ANY)
    return pl.pallas_call(
        functools.partial(kernel, nc, ns),
        out_shape=(
            jax.ShapeDtypeStruct((conds, ROWS, ny), F32),
            jax.ShapeDtypeStruct((ROWS, ny), F32),
        ),
        in_specs=[any_space] * 8,
        out_specs=(any_space, any_space),
        scratch_shapes=[
            vmem(conds, 3, ROWS, ny),
            vmem(conds, 2, ROWS, ny),
            vmem(conds, ROWS, ny, dtype=jnp.int32),
            vmem(3, ROWS, ny),
            vmem(ROWS, ny, dtype=jnp.int32),
            pltpu.SMEM((1, nc * conds), jnp.int32),
            vmem(2, conds, 3, HALO, ny),
            vmem(2, conds, 2, HALO, ny),
            vmem(2, conds, HALO, ny, dtype=jnp.int32),
            vmem(2, 3, HALO, ny),
            state(),
            state(),
            state(),
            state(),
            state(),
            per_cond(),
            per_cond(),
            per_cond(),
            grid(),
            grid(),
            grid(),
            grid(),
            vmem(blocks, 24, LANES),
            vmem(nc, blocks // nc, 24, LANES),
            vmem(blocks, 24, LANES),
            vmem(blocks, 8, LANES),
            vmem(blocks, 8, LANES),
            grid(),
            grid(),
            grid(),
            grid(),
            vmem(blocks + 2, TALL + 8, LANES),
            grid(),
            vmem(ns, 8, LANES),
            vmem(conds, ROWS, ny),
            vmem(ROWS, ny),
            dma((5 + 3 * conds,)),
            dma((2,)),
            dma((2, rims)),
            dma((2, rims)),
            dma(()),
            dma(()),
            dma((3,)),
            dma(()),
            dma(()),
            dma(()),
            dma(()),
            dma(()),
            pltpu.SemaphoreType.REGULAR((4,)),
        ],
        compiler_params=pltpu.CompilerParams(
            collective_id=0, has_side_effects=True, vmem_limit_bytes=56 << 20
        ),
        cost_estimate=pl.CostEstimate(
            flops=20_000_000, bytes_accessed=4_000_000, transcendentals=0
        ),
        name="morphology",
    )(flow, forcing, wet, depth, limiter, weights.reshape(1, -1), bed, diffusivity)


def solution(mesh):
    in_specs = (
        P("cond", None, "space", None),
        P("cond", None, "space", None),
        P("cond", "space", None),
        P("space", None),
        P("space", None),
        P(),
        P("space", None),
        P("space", None),
    )
    out_specs = (P("cond", "space", None), P("space", None))
    body = functools.partial(local, mesh.shape["cond"], mesh.shape["space"])
    return jax.shard_map(body, mesh=mesh, in_specs=in_specs, out_specs=out_specs, check_vma=False)
```

```python
import functools

import jax
import jax.numpy as jnp
from jax import lax
from jax.experimental import pallas as pl
from jax.experimental.pallas import tpu as pltpu
from jax.sharding import PartitionSpec as P

MESH = pl.DeviceIdType.MESH
F32 = jnp.float32

STEPS = 4
TIME_STEP = 0.4
GRAVITY = 1.0
FRICTION = 0.1
TRANSPORT_BASE = 0.5
MORPH_FACTOR = 1.0
SLOPE_COEFF = 1.0

LANES = 128
ROWS = 16
HALO = 8
TALL = ROWS + 2 * HALO
HALF_STEPS = 2 * STEPS
EDGE = 18
GROUP = 8


def kernel(
    nc,
    ns,
    flow,
    forcing,
    wet,
    depth,
    limiter,
    weights,
    bed,
    diffusivity,
    surface_twice,
    bed_twice,
    flow_own,
    force_own,
    wet_own,
    grid_own,
    lim_own,
    w_own,
    flow_rim,
    force_rim,
    wet_rim,
    grid_rim,
    eta,
    vel_a,
    vel_b,
    dva,
    dvb,
    mask,
    fa,
    fb,
    dep,
    lim,
    qa,
    qb,
    outbox,
    inbox,
    in_up,
    in_dn,
    diff,
    kd,
    kr,
    kl,
    b,
    y,
    slice_b,
    slice_y,
    slice_kd,
    slice_kr,
    slice_kl,
    sums,
    totals,
    load_sem,
    rim_send,
    rim_recv,
    rs_send,
    rs_recv,
    up_recv,
    dn_recv,
    ag_send,
    ag_recv,
    sum_send,
    sum_recv,
    known,
):
    c = lax.axis_index("cond")
    s = lax.axis_index("space")
    blocks = kd.shape[0] - 2
    conds = flow.shape[0]
    share = blocks // nc
    lane = lax.broadcasted_iota(jnp.int32, (8, LANES), 1)
    sub = lax.broadcasted_iota(jnp.int32, (8, LANES), 0)

    def wide(pattern, n):
        return pattern if n == 1 else jnp.concatenate([pattern] * n, 0)

    def each_block(body, size=GROUP):
        for at in range(1, blocks + 1, size):
            for store in [body(k) for k in range(at, at + size)]:
                store()

    loads = []

    def load(src, dst):
        copy = pltpu.make_async_copy(src, dst, load_sem.at[len(loads)])
        copy.start()
        loads.append(copy)
        return copy

    l_depth = load(depth, grid_own.at[0])
    l_cond = []
    for j in range(conds):
        l_cond.append(
            [
                load(flow.at[j], flow_own.at[j]),
                load(forcing.at[j], force_own.at[j]),
                load(wet.at[j], wet_own.at[j]),
            ]
        )
    l_w = load(weights, w_own)
    l_lim = load(limiter, lim_own)
    l_diff = load(diffusivity, grid_own.at[1])
    l_bed = load(bed, grid_own.at[2])

    for ref in (in_up, in_dn):
        ref[:, :, 0:3] = jnp.zeros((nc, share + 1, 3, LANES), F32)

    near_space = [(c, lax.rem(s + d, ns)) for d in (1, ns - 1)]
    near_cond = [(c + 1 - 2 * lax.rem(c, 2), s)]
    near_cond += [(lax.rem(c + d, nc), s) for d in (2, nc - 2)]
    near = near_space + near_cond
    barrier = pltpu.get_barrier_semaphore()
    for peer in near:
        pl.semaphore_signal(barrier, inc=1, device_id=peer, device_id_type=MESH)

    for ref in (eta, dvb):
        for block in (0, blocks + 1):
            ref[:, block] = jnp.zeros((conds * HALF_STEPS, TALL, LANES), F32)
    for ref in (qb, diff, b, kd, kr, kl):
        for block in (0, blocks + 1):
            ref[block] = jnp.zeros(ref.shape[1:], F32)
    for block in range(1, blocks + 1):
        qa[block] = jnp.zeros((TALL, LANES), F32)
        qb[block] = jnp.zeros((TALL, LANES), F32)
    pl.semaphore_wait(barrier, len(near))

    slow = lax.rem(s, 2)
    fast = 1 - slow

    def has(side):
        return jnp.where(side == 0, s > 0, s < ns - 1)

    def rim_copies(side, slot):
        peer = (c, s - 1 + 2 * side)

        def rows(count):
            if side == 0:
                return slice(0, count), slice(0, count)
            return slice(ROWS - count, ROWS), slice(HALO - count, HALO)

        pairs = []

        def add(src, dst, count, *index):
            here, there = rows(count)
            pairs.append((src.at[(*index, here)], dst.at[(slot, *index, there)]))

        def add_grid(src, at, count):
            here, there = rows(count)
            pairs.append((src.at[here], grid_rim.at[slot, at, there]))

        add_grid(depth, 0, HALO)
        for j in range(conds):
            here, there = rows(HALO)
            pairs.append((flow.at[j, 0:2, here], flow_rim.at[slot, j, 0:2, there]))
            add(flow, flow_rim, HALO - 1, j, 2)
            add(forcing, force_rim, HALO - 1, j, 0)
            add(forcing, force_rim, HALO - 2, j, 1)
            add(wet, wet_rim, HALO - 1, j)
            if j == 0:
                add_grid(diffusivity, 1, 2)
                add_grid(bed, 2, 2)

        def copy(i):
            src, dst = pairs[i]
            return pltpu.make_async_remote_copy(
                src,
                dst,
                rim_send.at[side, i],
                rim_recv.at[slot, i],
                device_id=peer,
                device_id_type=MESH,
            )

        return [functools.partial(copy, i) for i in range(len(pairs))]

    per = 5
    rims_grid = (1 + per, 2 + per)

    def rims_cond(j):
        first_one = 1 if j == 0 else 3 + per * j
        return range(first_one, first_one + per)

    def start_rims(side):
        for copy in rim_copies(side, 1 - side):
            copy().start()

    def wait_rims(side, which):
        for value in (0, 1):

            def wait(value=value):
                copies = rim_copies(value, value)
                for i in which:
                    copies[i]().wait_recv()

            pl.when(jnp.logical_and(side == value, has(side)))(wait)

    for order in (0, 1):
        for side in (order, 1 - order):
            go = jnp.logical_and(slow == order, has(side))
            pl.when(go)(functools.partial(start_rims, side))

    def tell(step, peers):
        for peer in peers:
            pl.semaphore_signal(
                known.at[step], inc=1, device_id=peer, device_id_type=MESH
            )
        return len(peers)

    def ring(d):
        return [(c, lax.rem(s + d, ns)), (c, lax.rem(s + ns - d, ns))]

    n0 = tell(0, near)

    def columns(k):
        return slice((k - 1) * LANES, k * LANES)

    def fill_grid(src, dst, rows, real=None):
        def body(k):
            value = src[:, columns(k)]
            if real is not None:
                value = jnp.where(real, value, jnp.zeros_like(value))

            def store():
                dst[k, rows, :] = value

            return store

        each_block(body)

    def fill_cond(j, flow_src, force_src, wet_src, rows, real=None):
        at0 = j * HALF_STEPS

        def body(k):
            at = columns(k)

            def get(value):
                if real is None:
                    return value
                return jnp.where(real, value, jnp.zeros_like(value))

            d = dep[k, rows, :]
            e = get(flow_src[0, :, at])
            u = get(flow_src[1, :, at])
            v = get(flow_src[2, :, at])
            m = get(wet_src[:, at]).astype(F32) * (0.5 * TIME_STEP)
            force_a = 2.0 * m * get(force_src[0, :, at])
            force_b = 2.0 * m * get(force_src[1, :, at])

            def store():
                eta[at0, k, rows, :] = e
                vel_a[at0, k, rows, :] = u
                vel_b[at0, k, rows, :] = v
                dva[at0, k, rows, :] = d * u
                dvb[at0, k, rows, :] = d * v
                mask[j, k, rows, :] = m
                fa[j, k, rows, :] = force_a
                fb[j, k, rows, :] = force_b

            return store

        each_block(body, GROUP // 2)

    own = pl.ds(HALO, ROWS)
    l_depth.wait()
    fill_grid(grid_own.at[0], dep, own)

    def advance(j, t, k, start, n):
        at = j * HALF_STEPS + t
        first_lane, last_lane = wide(lane, n) == 0, wide(lane, n) == LANES - 1
        rows, up, dn = (pl.ds(start + d, 8 * n) for d in (0, -1, 1))

        def across(ref):
            here = ref[at, k, rows, :]
            right = jnp.where(first_lane, ref[at, k + 1, rows, :], here)
            left = jnp.where(last_lane, ref[at, k - 1, rows, :], here)
            return here, pltpu.roll(right, LANES - 1, 1) - pltpu.roll(left, 1, 1)

        e, e_across = across(eta)
        _, h_across = across(dvb)
        m = mask[j, k, rows, :]
        keep = 1.0 - (2.0 * FRICTION) * m
        e_next = e - m * (dva[at, k, dn, :] - dva[at, k, up, :] + h_across)
        slope = GRAVITY * m
        u_next = keep * vel_a[at, k, rows, :] + fa[j, k, rows, :]
        u_next = u_next - slope * (eta[at, k, dn, :] - eta[at, k, up, :])
        v_next = keep * vel_b[at, k, rows, :] + fb[j, k, rows, :] - slope * e_across
        return e_next, u_next, v_next

    def put(j, t, k, start, n, state):
        at = j * HALF_STEPS + t
        rows = pl.ds(start, 8 * n)
        e, u, v = state
        d = dep[k, rows, :]
        eta[at, k, rows, :] = e
        vel_a[at, k, rows, :] = u
        vel_b[at, k, rows, :] = v
        dva[at, k, rows, :] = d * u
        dvb[at, k, rows, :] = d * v

    def first(j, t, start, n):
        def body(k):
            state = advance(j, t - 1, k, start, n)
            return lambda: put(j, t, k, start, n, state)

        each_block(body, GROUP // n)

    def second(j, t, start, n, weight, valid=None, last=None):
        def body(k):
            at = j * HALF_STEPS + t - 2
            rows = pl.ds(start, 8 * n)
            e, u, v = advance(j, t - 1, k, start, n)
            e = eta[at, k, rows, :] + e
            u = 0.5 * (vel_a[at, k, rows, :] + u)
            v = 0.5 * (vel_b[at, k, rows, :] + v)
            energy = u * u + v * v
            factor = weight * (TRANSPORT_BASE + energy)
            factor = factor / (1.0 + lim[k, rows, :] * energy)
            add_a, add_b = u * factor, v * factor
            if valid is not None:
                add_a = jnp.where(valid, add_a, 0.0)
                add_b = jnp.where(valid, add_b, 0.0)
            sum_a = qa[k, rows, :] + add_a
            sum_b = qb[k, rows, :] + add_b

            def store():
                if last is None:
                    put(j, t, k, start, n, (0.5 * e, u, v))
                else:
                    surface_twice[j, last, columns(k)] = e
                qa[k, rows, :] = sum_a
                qb[k, rows, :] = sum_b

            return store

        each_block(body, GROUP // n)

    def interior(j, weight):
        for t in range(1, HALF_STEPS):
            count = ROWS - 2 * t
            n = -(-count // 8)
            if t % 2:
                first(j, t, HALO + t, n)
            else:
                valid = None
                if count % 8:
                    place = jnp.concatenate([sub + 8 * i for i in range(n)], 0)
                    valid = place < count
                second(j, t, HALO + t, n, weight, valid)

    def side_steps(j, side, weight):
        def pair(p, carry):
            t = 2 * p + 1
            first(j, t, jnp.where(side == 0, t, 24 - t), 1)
            t = 2 * p + 2
            second(j, t, jnp.where(side == 0, t, 24 - t), 1, weight)
            return carry

        lax.fori_loop(0, STEPS - 1, pair, 0)
        t = HALF_STEPS - 1
        first(j, t, jnp.where(side == 0, t, 24 - t), 1)
        rows = pl.ds(pl.multiple_of(8 * side, 8), 8)
        second(j, t + 1, pl.multiple_of(8 + 8 * side, 8), 1, weight, last=rows)

    l_w.wait()
    weight = [w_own[0, conds * c + j].astype(F32) for j in range(conds)]
    w_sum = w_own[0, 0]
    for i in range(1, nc * conds):
        w_sum = w_sum + w_own[0, i]
    w_sum = w_sum.astype(F32)

    def lim_rows():
        l_lim.wait()

        def body(k):
            value = lim_own[:, columns(k)].astype(F32)

            def store():
                lim[k, own, :] = value
                lim[k, 0:8, :] = jnp.zeros((8, LANES), F32)
                lim[k, 24:32, :] = jnp.zeros((8, LANES), F32)

            return store

        each_block(body)

    lim_rows()
    for j in range(conds):
        for copy in l_cond[j]:
            copy.wait()
        fill_cond(j, flow_own.at[j], force_own.at[j], wet_own.at[j], own)
        interior(j, weight[j])

    pl.semaphore_wait(known.at[0], n0)
    n1 = tell(1, near + ring(2))
    l_diff.wait()
    l_bed.wait()
    fill_grid(grid_own.at[1], diff, own)

    def rim_rows(side):
        return pl.ds(pl.multiple_of(24 * side, 8), 8)

    def side_grid(side):
        fill_grid(grid_rim.at[side, 0], dep, rim_rows(side), has(side))

    def side_cond(side, j):
        fill_cond(
            j,
            flow_rim.at[side, j],
            force_rim.at[side, j],
            wet_rim.at[side, j],
            rim_rows(side),
            has(side),
        )
        side_steps(j, side, weight[j])

    wait_rims(fast, (0,))
    side_grid(fast)
    for j in range(conds):
        wait_rims(fast, rims_cond(j))
        side_cond(fast, j)
    wait_rims(fast, rims_grid)
    fill_grid(grid_rim.at[fast, 1], diff, rim_rows(fast))

    pl.semaphore_wait(known.at[1], n1)
    n2 = tell(2, near + ring(4))

    wait_rims(slow, (0,))
    side_grid(slow)
    wait_rims(slow, rims_cond(0))
    side_cond(slow, 0)
    wait_rims(slow, rims_grid)
    fill_grid(grid_rim.at[slow, 1], diff, rim_rows(slow), has(slow))

    first_lane3 = wide(lane, 3) == 0
    last_lane3 = wide(lane, 3) == LANES - 1

    def faces(k):
        rows, dn = pl.ds(7, 24), pl.ds(8, 24)

        def face(p, q):
            total = p + q
            return SLOPE_COEFF * p * q / jnp.where(total > 0.0, total, 1.0)

        d = diff[k, rows, :]
        right = jnp.where(first_lane3, diff[k + 1, rows, :], d)
        left = jnp.where(last_lane3, diff[k - 1, rows, :], d)
        f_dn = face(d, diff[k, dn, :])
        f_right = face(d, pltpu.roll(right, LANES - 1, 1))
        f_left = face(d, pltpu.roll(left, 1, 1))

        def store():
            kd[k, rows, :] = f_dn
            kr[k, rows, :] = f_right
            kl[k, rows, :] = f_left

        return store

    each_block(faces, GROUP // 4)
    pl.semaphore_wait(known.at[2], n2)
    n3 = tell(3, ring(8))

    right_part = lane < LANES // 2

    def beside(left, right):
        return jnp.where(wide(right_part, left.shape[0] // 8), right, left)

    def bed_block(k):
        at = pl.ds(pl.multiple_of(k * LANES, LANES), LANES)
        return (
            grid_rim[0, 2, :, at],
            grid_own[2, :, at],
            grid_rim[1, 2, :, at],
        )

    before = lax.max(share * c - 1, 0)
    after = lax.min(share * (c + 1), blocks - 1)
    beds = [bed_block(share * c + r) for r in range(share)]
    beds.append(tuple(map(beside, bed_block(before), bed_block(after))))
    for r, (above, own_rows, below) in enumerate(beds):
        slice_b[r, 0:8] = jnp.where(s > 0, above, 0.0)
        slice_b[r, 8:24] = own_rows
        slice_b[r, 24:32] = jnp.where(s < ns - 1, below, 0.0)
    for src, dst in ((kd, slice_kd), (kr, slice_kr), (kl, slice_kl)):
        for r in range(share):
            dst[r] = src[share * c + 1 + r]
        dst[share] = beside(src[share * c], src[share * (c + 1) + 1])
    pl.semaphore_wait(known.at[3], n3)

    for j in range(1, conds):
        wait_rims(slow, rims_cond(j))
        side_cond(slow, j)

    scale = (-0.5 * MORPH_FACTOR) / w_sum

    for k in range(1, blocks + 1):
        for ref in (qa, qb):
            ref[k, 0:8, :] = jnp.zeros((8, LANES), F32)
            ref[k, 24:32, :] = jnp.zeros((8, LANES), F32)

    def divergence(k):
        rows, up, dn = pl.ds(7, 24), pl.ds(6, 24), pl.ds(8, 24)
        here = qb[k, rows, :]
        right = jnp.where(first_lane3, qb[k + 1, rows, :], here)
        left = jnp.where(last_lane3, qb[k - 1, rows, :], here)
        total = pltpu.roll(right, LANES - 1, 1) - pltpu.roll(left, 1, 1)
        total = total + (qa[k, dn, :] - qa[k, up, :])
        total = scale * total

        def store():
            outbox[(k - 1) // share, (k - 1) % share] = total

        return store

    each_block(divergence, GROUP // 2)

    nothing = jnp.zeros((24, LANES), F32)
    for to in range(nc):
        left = outbox[to - 1, share - 1] if to > 0 else nothing
        right = outbox[to + 1, 0] if to < nc - 1 else nothing
        outbox[to, share] = beside(left, right)

    def remote(src, dst, send, recv, peer):
        copy = pltpu.make_async_remote_copy(
            src, dst, send, recv, device_id=peer, device_id_type=MESH
        )
        copy.start()

    def arrive(ref, sem):
        pltpu.make_async_copy(ref, ref, sem).wait()

    def edges(side):
        rows = slice(0, 3) if side == 0 else slice(EDGE - 3, EDGE)
        land, recv = (in_dn, dn_recv) if side == 0 else (in_up, up_recv)
        for d in range(nc):
            peer = lax.rem(c + d, nc)
            remote(
                outbox.at[peer, :, rows],
                land.at[d, :, 0:3],
                rs_send.at[1 + side],
                recv,
                (peer, s - 1 + 2 * side),
            )

    pl.when(jnp.logical_and(slow == 0, s > 0))(lambda: edges(0))
    pl.when(jnp.logical_and(slow == 1, s < ns - 1))(lambda: edges(1))
    for d in range(1, nc):
        peer = lax.rem(c + d, nc)
        remote(
            outbox.at[peer, :, 0:EDGE],
            inbox.at[d, :, 0:EDGE],
            rs_send.at[0],
            rs_recv,
            (peer, s),
        )
    pl.when(slow == 1)(lambda: edges(0))
    pl.when(slow == 0)(lambda: edges(1))

    landed = inbox.at[1:nc, :, 0:EDGE]
    edge_up, edge_dn = in_up.at[:, :, 0:3], in_dn.at[:, :, 0:3]
    arrive(landed, rs_recv)
    total = [outbox[c, :, 0:16], outbox[c, :, 16:EDGE]]
    for d in range(1, nc):
        total[0] = total[0] + inbox[d, :, 0:16]
        total[1] = total[1] + inbox[d, :, 16:EDGE]
    slice_b[:, 7:23] = slice_b[:, 7:23] + total[0]
    slice_b[:, 23:25] = slice_b[:, 23:25] + total[1]
    pl.when(s > 0)(lambda: arrive(edge_up, up_recv))
    pl.when(s < ns - 1)(lambda: arrive(edge_dn, dn_recv))
    for land, start in ((in_up, 6), (in_dn, 23)):
        extra = land[0, :, 0:3]
        for d in range(1, nc):
            extra = extra + land[d, :, 0:3]
        slice_b[:, start : start + 3] = slice_b[:, start : start + 3] + extra

    def image_of(get, face_dn, face_right, face_left, left, right, n):
        rows, up, dn = (slice(8 + d, 8 + d + 8 * n) for d in (0, -1, 1))
        first_lane, last_lane = wide(lane, n) == 0, wide(lane, n) == LANES - 1
        here = get(rows)
        to_right = jnp.where(first_lane, right(rows), here)
        to_left = jnp.where(last_lane, left(rows), here)
        to_dn, to_up = here - get(dn), here - get(up)
        to_right = here - pltpu.roll(to_right, LANES - 1, 1)
        to_left = here - pltpu.roll(to_left, 1, 1)
        f_dn, f_right = face_dn(rows) * to_dn, face_right(rows) * to_right
        image = f_dn + face_dn(up) * to_up + f_right + face_left(rows) * to_left
        return here, image, f_dn * to_dn + f_right * to_right

    def fold(value):
        return value[0:8] + value[8:16]

    def rows_of(ref, k):
        return lambda rows: ref[k, rows, :]

    zero = jnp.zeros((8, LANES), F32)
    bb, bl, ll, lyl = zero, zero, zero, zero
    images = []
    for r in range(share + 1):
        here, image, energy = image_of(
            rows_of(slice_b, r),
            rows_of(slice_kd, r),
            rows_of(slice_kr, r),
            rows_of(slice_kl, r),
            rows_of(slice_b, r - 1 if r else share),
            rows_of(slice_b, min(r + 1, share)),
            3,
        )
        images.append(image)
        if r < share:
            bb, bl, ll = bb + fold(here * here), bl + fold(energy), ll + fold(image * image)
    for r in range(share):
        slice_y[r] = images[r]
        here = images[r][0:16]
        right = jnp.where(wide(lane, 2) == 0, images[r + 1][0:16], here)
        to_right = here - pltpu.roll(right, LANES - 1, 1)
        to_dn = here - slice_y[r, 1:17]
        f_dn, f_right = slice_kd[r, own] * to_dn, slice_kr[r, own] * to_right
        lyl = lyl + fold(f_dn * to_dn + f_right * to_right)
    tile = zero
    for i, value in enumerate((bb, bl, ll, lyl)):
        tile = jnp.where(sub == i, jnp.sum(value, 0, keepdims=True), tile)

    half = ns // 2
    sums[0] = tile
    for e in range(2):
        for d in range(nc):
            if d or e:
                peer = (lax.rem(c + d, nc), lax.rem(s + half * e, ns))
                at = nc * e + d
                remote(sums.at[0], sums.at[at], sum_send.at[0], sum_recv.at[0], peer)
    mine = pl.ds(share * c + 1, share)
    b_own = slice_b.at[0:share, 7:25]
    for d in range(1, nc):
        peer = (lax.rem(c + d, nc), s)
        remote(b_own, b.at[mine, 7:25], ag_send, ag_recv, peer)
    b[mine, 7:23] = slice_b[0:share, 7:23]
    b[mine, 23:25] = slice_b[0:share, 23:25]

    others = sums.at[1 : 2 * nc]
    arrive(others, sum_recv.at[0])
    totals[0] = jnp.sum(sums[...], 0)
    base, place = s - lax.rem(s, half), lax.rem(s, half)
    for d in range(1, half):
        peer = (c, base + lax.rem(place + d, half))
        remote(totals.at[0], totals.at[d], sum_send.at[1], sum_recv.at[1], peer)

    gathered = b.at[1 : blocks + 1 - share, 7:25]
    arrive(gathered, ag_recv)

    def strip(k):
        _, image, _ = image_of(
            rows_of(b, k),
            rows_of(kd, k),
            rows_of(kr, k),
            rows_of(kl, k),
            rows_of(b, k - 1),
            rows_of(b, k + 1),
            2,
        )

        def store():
            y[k, 0:16] = image

        return store

    each_block(strip, GROUP // 2)
    halves = totals.at[1:half]
    arrive(halves, sum_recv.at[1])
    total = jnp.sum(jnp.sum(totals[...], 0), 1, keepdims=True)
    s_bb, s_bl, s_ll, s_lyl = (total[i : i + 1] for i in range(4))
    m1, m2, m3 = s_bl / s_bb, s_ll / s_bb, s_lyl / s_bb
    alpha0 = 1.0 / (1.0 + m1)
    beta = (m2 - m1 * m1) * alpha0 * alpha0
    p_b = m1 * alpha0 + beta
    p_l = alpha0
    pp = p_b * p_b - 2.0 * p_b * p_l * m1 + p_l * p_l * m2
    plp = p_b * p_b * m1 - 2.0 * p_b * p_l * m2 + p_l * p_l * m3
    alpha1 = beta / (pp + plp)
    x_b = alpha0 + alpha1 * p_b
    x_l = -alpha1 * p_l

    x_b, x_l = 2.0 * x_b, 2.0 * x_l
    for k in range(1, blocks + 1):
        bed_twice[:, columns(k)] = x_b * b[k, own] + x_l * y[k, 0:16]

    for side in (0, 1):

        def sent(side=side):
            for copy in rim_copies(side, 1 - side):
                copy().wait_send()
            arrive(edge_up, rs_send.at[1 + side])

        pl.when(has(side))(sent)
    arrive(landed, rs_send.at[0])
    arrive(gathered, ag_send)
    arrive(others, sum_send.at[0])
    arrive(halves, sum_send.at[1])


def local(nc, ns, flow, forcing, wet, depth, limiter, weights, bed, diffusivity):
    conds, ny = flow.shape[0], flow.shape[-1]
    blocks = ny // LANES
    dma = pltpu.SemaphoreType.DMA

    def vmem(*shape, dtype=F32):
        return pltpu.VMEM(shape, dtype)

    def state():
        return vmem(conds * HALF_STEPS, blocks + 2, TALL, LANES)

    def per_cond():
        return vmem(conds, blocks + 2, TALL, LANES)

    def grid():
        return vmem(blocks + 2, TALL, LANES)

    share = blocks // nc
    rims = 3 + 5 * conds
    any_space = pl.BlockSpec(memory_space=pl.ANY)
    in_vmem = pl.BlockSpec(memory_space=pltpu.VMEM)
    surface_twice, bed_twice = pl.pallas_call(
        functools.partial(kernel, nc, ns),
        out_shape=(
            pltpu.VMEM((conds, ROWS, ny), F32),
            pltpu.VMEM((ROWS, ny), F32),
        ),
        in_specs=[any_space] * 8,
        out_specs=(in_vmem, in_vmem),
        scratch_shapes=[
            vmem(conds, 3, ROWS, ny),
            vmem(conds, 2, ROWS, ny),
            vmem(conds, ROWS, ny, dtype=jnp.int32),
            vmem(3, ROWS, ny),
            vmem(ROWS, ny, dtype=jnp.int32),
            pltpu.SMEM((1, nc * conds), jnp.int32),
            vmem(2, conds, 3, HALO, ny),
            vmem(2, conds, 2, HALO, ny),
            vmem(2, conds, HALO, ny, dtype=jnp.int32),
            vmem(2, 3, HALO, ny),
            state(),
            state(),
            state(),
            state(),
            state(),
            per_cond(),
            per_cond(),
            per_cond(),
            grid(),
            grid(),
            grid(),
            grid(),
            vmem(nc, share + 1, 24, LANES),
            vmem(nc, share + 1, 24, LANES),
            vmem(nc, share + 1, 8, LANES),
            vmem(nc, share + 1, 8, LANES),
            grid(),
            grid(),
            grid(),
            grid(),
            grid(),
            vmem(blocks + 1, ROWS, LANES),
            vmem(share + 1, TALL + 8, LANES),
            vmem(share, 24, LANES),
            vmem(share + 1, TALL, LANES),
            vmem(share + 1, TALL, LANES),
            vmem(share + 1, TALL, LANES),
            vmem(2 * nc, 8, LANES),
            vmem(ns // 2, 8, LANES),
            dma((5 + 3 * conds,)),
            dma((2, rims)),
            dma((2, rims)),
            dma((3,)),
            dma(()),
            dma(()),
            dma(()),
            dma(()),
            dma(()),
            dma((2,)),
            dma((2,)),
            pltpu.SemaphoreType.REGULAR((4,)),
        ],
        compiler_params=pltpu.CompilerParams(
            collective_id=0, has_side_effects=True, vmem_limit_bytes=58 << 20
        ),
        cost_estimate=pl.CostEstimate(
            flops=20_000_000, bytes_accessed=4_000_000, transcendentals=0
        ),
        name="morphology",
    )(flow, forcing, wet, depth, limiter, weights.reshape(1, -1), bed, diffusivity)
    return 0.5 * surface_twice, 0.5 * bed_twice


def solution(mesh):
    in_specs = (
        P("cond", None, "space", None),
        P("cond", None, "space", None),
        P("cond", "space", None),
        P("space", None),
        P("space", None),
        P(),
        P("space", None),
        P("space", None),
    )
    out_specs = (P("cond", "space", None), P("space", None))
    body = functools.partial(local, mesh.shape["cond"], mesh.shape["space"])
    return jax.shard_map(body, mesh=mesh, in_specs=in_specs, out_specs=out_specs, check_vma=False)
```

```python
import functools

import jax
import jax.numpy as jnp
from jax import lax
from jax.experimental import pallas as pl
from jax.experimental.pallas import tpu as pltpu
from jax.sharding import PartitionSpec as P

MESH = pl.DeviceIdType.MESH
F32 = jnp.float32

STEPS = 4
TIME_STEP = 0.4
GRAVITY = 1.0
FRICTION = 0.1
TRANSPORT_BASE = 0.5
MORPH_FACTOR = 1.0
SLOPE_COEFF = 1.0

LANES = 128
ROWS = 16
HALO = 8
TALL = ROWS + 2 * HALO
HALF_STEPS = 2 * STEPS
STATES = HALF_STEPS + 1
EDGE = 18
GROUP = 8


def kernel(
    nc,
    ns,
    flow,
    forcing,
    wet,
    depth,
    limiter,
    weights,
    bed,
    diffusivity,
    surface_twice,
    bed_twice,
    flow_own,
    force_own,
    wet_own,
    grid_own,
    lim_own,
    w_own,
    flow_rim,
    force_rim,
    wet_rim,
    grid_rim,
    eta,
    vel_a,
    vel_b,
    dva,
    dvb,
    mask,
    fa,
    fb,
    dep,
    lim,
    qa,
    qb,
    outbox,
    inbox,
    in_up,
    in_dn,
    diff,
    kd,
    kr,
    kl,
    b,
    y,
    slice_b,
    slice_y,
    slice_kd,
    slice_kr,
    slice_kl,
    sums,
    totals,
    load_sem,
    rim_send,
    rim_recv,
    rs_send,
    rs_recv,
    up_recv,
    dn_recv,
    ag_send,
    ag_recv,
    sum_send,
    sum_recv,
    known,
):
    c = lax.axis_index("cond")
    s = lax.axis_index("space")
    blocks = kd.shape[0] - 2
    conds = flow.shape[0]
    share = blocks // nc
    lane = lax.broadcasted_iota(jnp.int32, (8, LANES), 1)
    sub = lax.broadcasted_iota(jnp.int32, (8, LANES), 0)

    def wide(pattern, n):
        return pattern if n == 1 else jnp.concatenate([pattern] * n, 0)

    def each_block(body, size=GROUP):
        for at in range(1, blocks + 1, size):
            for store in [body(k) for k in range(at, at + size)]:
                store()

    for ref in (in_up, in_dn):
        ref[:, :, 0:3] = jnp.zeros((nc, share + 1, 3, LANES), F32)

    near_space = [(c, lax.rem(s + d, ns)) for d in (1, ns - 1)]
    near_cond = [(c + 1 - 2 * lax.rem(c, 2), s)]
    near_cond += [(lax.rem(c + d, nc), s) for d in (2, nc - 2)]
    near = near_space + near_cond
    barrier = pltpu.get_barrier_semaphore()
    for peer in near:
        pl.semaphore_signal(barrier, inc=1, device_id=peer, device_id_type=MESH)

    pl.semaphore_wait(barrier, len(near))

    slow = lax.rem(s, 2)
    fast = 1 - slow

    def has(side):
        return jnp.where(side == 0, s > 0, s < ns - 1)

    def rim_copies(side, slot):
        peer = (c, s - 1 + 2 * side)

        def rows(count):
            if side == 0:
                return slice(0, count), slice(0, count)
            return slice(ROWS - count, ROWS), slice(HALO - count, HALO)

        def grid_pair(src, at, count):
            here, there = rows(count)
            return src.at[here], grid_rim.at[slot, at, there]

        def cond_pair(src, dst, count, *index):
            here, there = rows(count)
            return src.at[(*index, here)], dst.at[(slot, *index, there)]

        def copy(i, pair):
            return pltpu.make_async_remote_copy(
                *pair,
                rim_send.at[side, i],
                rim_recv.at[slot, i],
                device_id=peer,
                device_id_type=MESH,
            )

        def of_grid(at):
            src, count = ((depth, HALO), (diffusivity, 2), (bed, 2))[at]
            return copy(at, grid_pair(src, at, count))

        def of_cond(j):
            here, there = rows(HALO)
            pairs = [
                (flow.at[j, 0:2, here], flow_rim.at[slot, j, 0:2, there]),
                cond_pair(flow, flow_rim, HALO - 1, j, 2),
                cond_pair(forcing, force_rim, HALO - 1, j, 0),
                cond_pair(forcing, force_rim, HALO - 2, j, 1),
                cond_pair(wet, wet_rim, HALO - 1, j),
            ]
            return [copy(3 + 5 * j + i, pair) for i, pair in enumerate(pairs)]

        return of_grid, of_cond

    def start_rims(side):
        of_grid, of_cond = rim_copies(side, 1 - side)
        of_grid(0).start()
        for copy in of_cond(0):
            copy.start()
        of_grid(1).start()
        of_grid(2).start()
        for j in range(1, conds):
            for copy in of_cond(j):
                copy.start()

    def by_side(side, body):
        for value in (0, 1):
            real = jnp.logical_and(side == value, has(value))
            pl.when(real)(functools.partial(body, *rim_copies(value, value)))

    def wait_grid(side, *which):
        def wait(of_grid, of_cond):
            for at in which:
                of_grid(at).wait_recv()

        by_side(side, wait)

    def wait_cond(side, j):
        def wait(of_grid, of_cond):
            for copy in of_cond(j):
                copy.wait_recv()

        by_side(side, wait)

    for order in (0, 1):
        for side in (order, 1 - order):
            go = jnp.logical_and(slow == order, has(side))
            pl.when(go)(functools.partial(start_rims, side))

    def loads_grid():
        pairs = [
            (depth, grid_own.at[0]),
            (weights, w_own),
            (limiter, lim_own),
            (diffusivity, grid_own.at[1]),
            (bed, grid_own.at[2]),
        ]
        return [
            pltpu.make_async_copy(src, dst, load_sem.at[i])
            for i, (src, dst) in enumerate(pairs)
        ]

    def loads_cond(j):
        pairs = [
            (flow.at[j], flow_own.at[j]),
            (forcing.at[j], force_own.at[j]),
            (wet.at[j], wet_own.at[j]),
        ]
        return [
            pltpu.make_async_copy(src, dst, load_sem.at[5 + 3 * j + i])
            for i, (src, dst) in enumerate(pairs)
        ]

    l_depth, l_w, l_lim, l_diff, l_bed = loads_grid()
    for copy in [l_depth, l_w, l_lim] + loads_cond(0):
        copy.start()
    for j in range(1, conds):
        for copy in loads_cond(j):
            copy.start()
    l_diff.start()
    l_bed.start()

    for ref in (eta, dvb):
        for block in (0, blocks + 1):
            ref[:, block] = jnp.zeros((conds * STATES, TALL, LANES), F32)
    for ref in (qb, diff, b, kd, kr, kl):
        for block in (0, blocks + 1):
            ref[block] = jnp.zeros(ref.shape[1:], F32)
    for block in range(1, blocks + 1):
        qa[block] = jnp.zeros((TALL, LANES), F32)
        qb[block] = jnp.zeros((TALL, LANES), F32)

    def tell(step, peers):
        for peer in peers:
            pl.semaphore_signal(
                known.at[step], inc=1, device_id=peer, device_id_type=MESH
            )
        return len(peers)

    def ring(d):
        return [(c, lax.rem(s + d, ns)), (c, lax.rem(s + ns - d, ns))]

    n0 = tell(0, near)

    def columns(k):
        return slice((k - 1) * LANES, k * LANES)

    def fill_grid(src, dst, rows, real=None):
        def body(k):
            value = src[:, columns(k)]
            if real is not None:
                value = jnp.where(real, value, jnp.zeros_like(value))

            def store():
                dst[k, rows, :] = value

            return store

        each_block(body)

    def fill_cond(j, flow_src, force_src, wet_src, rows, real=None):
        at0 = j * STATES

        def body(k):
            at = columns(k)

            def get(value):
                if real is None:
                    return value
                return jnp.where(real, value, jnp.zeros_like(value))

            d = dep[k, rows, :]
            e = get(flow_src[0, :, at])
            u = get(flow_src[1, :, at])
            v = get(flow_src[2, :, at])
            m = get(wet_src[:, at]).astype(F32) * (0.5 * TIME_STEP)
            force_a = 2.0 * m * get(force_src[0, :, at])
            force_b = 2.0 * m * get(force_src[1, :, at])

            def store():
                eta[at0, k, rows, :] = e
                vel_a[at0, k, rows, :] = u
                vel_b[at0, k, rows, :] = v
                dva[at0, k, rows, :] = d * u
                dvb[at0, k, rows, :] = d * v
                mask[j, k, rows, :] = m
                fa[j, k, rows, :] = force_a
                fb[j, k, rows, :] = force_b

            return store

        each_block(body, GROUP // 2)

    own = pl.ds(HALO, ROWS)
    l_depth.wait()
    fill_grid(grid_own.at[0], dep, own)

    def advance(j, t, k, start, n):
        at = j * STATES + t
        first_lane, last_lane = wide(lane, n) == 0, wide(lane, n) == LANES - 1
        rows, up, dn = (pl.ds(start + d, 8 * n) for d in (0, -1, 1))

        def across(ref):
            here = ref[at, k, rows, :]
            right = jnp.where(first_lane, ref[at, k + 1, rows, :], here)
            left = jnp.where(last_lane, ref[at, k - 1, rows, :], here)
            return here, pltpu.roll(right, LANES - 1, 1) - pltpu.roll(left, 1, 1)

        e, e_across = across(eta)
        _, h_across = across(dvb)
        m = mask[j, k, rows, :]
        keep = 1.0 - (2.0 * FRICTION) * m
        e_next = e - m * (dva[at, k, dn, :] - dva[at, k, up, :] + h_across)
        slope = GRAVITY * m
        u_next = keep * vel_a[at, k, rows, :] + fa[j, k, rows, :]
        u_next = u_next - slope * (eta[at, k, dn, :] - eta[at, k, up, :])
        v_next = keep * vel_b[at, k, rows, :] + fb[j, k, rows, :] - slope * e_across
        return e_next, u_next, v_next

    def put(j, t, k, start, n, state):
        at = j * STATES + t
        rows = pl.ds(start, 8 * n)
        e, u, v = state
        d = dep[k, rows, :]
        eta[at, k, rows, :] = e
        vel_a[at, k, rows, :] = u
        vel_b[at, k, rows, :] = v
        dva[at, k, rows, :] = d * u
        dvb[at, k, rows, :] = d * v

    def first(j, t, start, n):
        def body(k):
            state = advance(j, t - 1, k, start, n)
            return lambda: put(j, t, k, start, n, state)

        each_block(body, GROUP // n)

    def second(j, t, start, n, weight, valid=None):
        def body(k):
            at = j * STATES + t - 2
            rows = pl.ds(start, 8 * n)
            e, u, v = advance(j, t - 1, k, start, n)
            e = 0.5 * (eta[at, k, rows, :] + e)
            u = 0.5 * (vel_a[at, k, rows, :] + u)
            v = 0.5 * (vel_b[at, k, rows, :] + v)
            energy = u * u + v * v
            factor = weight * (TRANSPORT_BASE + energy)
            factor = factor / (1.0 + lim[k, rows, :] * energy)
            add_a, add_b = u * factor, v * factor
            if valid is not None:
                add_a = jnp.where(valid, add_a, 0.0)
                add_b = jnp.where(valid, add_b, 0.0)
            sum_a = qa[k, rows, :] + add_a
            sum_b = qb[k, rows, :] + add_b

            def store():
                put(j, t, k, start, n, (e, u, v))
                qa[k, rows, :] = sum_a
                qb[k, rows, :] = sum_b

            return store

        each_block(body, GROUP // n)

    def interior(j, weight):
        def pair(p, carry, n):
            t = 2 * p + 1
            first(j, t, HALO + t, n)
            place = jnp.concatenate([sub + 8 * i for i in range(n)], 0)
            second(j, t + 1, HALO + t + 1, n, weight, place < ROWS - 2 * (t + 1))
            return carry

        lax.fori_loop(0, 2, functools.partial(pair, n=2), 0)
        for p in range(2, STEPS - 1):
            pair(p, 0, 1)
        first(j, HALF_STEPS - 1, HALO + HALF_STEPS - 1, 1)

    def side_steps(j, side, weight):
        def pair(p, carry):
            t = 2 * p + 1
            first(j, t, jnp.where(side == 0, t, 24 - t), 1)
            t = 2 * p + 2
            second(j, t, jnp.where(side == 0, t, 24 - t), 1, weight)
            return carry

        lax.fori_loop(0, STEPS, pair, 0)
        rows = pl.ds(pl.multiple_of(8 * side, 8), 8)
        held = pl.ds(pl.multiple_of(8 + 8 * side, 8), 8)
        for k in range(1, blocks + 1):
            state = eta[j * STATES + HALF_STEPS, k, held, :]
            surface_twice[j, rows, columns(k)] = 2.0 * state

    l_w.wait()
    w_sum = w_own[0, 0]
    for i in range(1, nc * conds):
        w_sum = w_sum + w_own[0, i]
    w_sum = w_sum.astype(F32)

    def lim_rows():
        l_lim.wait()

        def body(k):
            value = lim_own[:, columns(k)].astype(F32)

            def store():
                lim[k, own, :] = value
                lim[k, 0:8, :] = jnp.zeros((8, LANES), F32)
                lim[k, 24:32, :] = jnp.zeros((8, LANES), F32)

            return store

        each_block(body)

    lim_rows()
    def weight_of(j):
        return w_own[0, conds * c + j].astype(F32)

    def start_cond(j, carry):
        for copy in loads_cond(j):
            copy.wait()
        fill_cond(j, flow_own.at[j], force_own.at[j], wet_own.at[j], own)
        interior(j, weight_of(j))
        return carry

    lax.fori_loop(0, conds, start_cond, 0)
    pl.semaphore_wait(known.at[0], n0)
    n1 = tell(1, near + ring(2))
    l_diff.wait()
    l_bed.wait()
    fill_grid(grid_own.at[1], diff, own)

    def rim_rows(side):
        return pl.ds(pl.multiple_of(24 * side, 8), 8)

    def side_grid(side):
        fill_grid(grid_rim.at[side, 0], dep, rim_rows(side), has(side))

    def side_cond(side, j):
        fill_cond(
            j,
            flow_rim.at[side, j],
            force_rim.at[side, j],
            wet_rim.at[side, j],
            rim_rows(side),
            has(side),
        )
        side_steps(j, side, weight_of(j))

    right_part = lane < LANES // 2

    def beside(left, right):
        return jnp.where(wide(right_part, left.shape[0] // 8), right, left)

    def remote(src, dst, send, recv, peer):
        copy = pltpu.make_async_remote_copy(
            src, dst, send, recv, device_id=peer, device_id_type=MESH
        )
        copy.start()

    def arrive(ref, sem):
        pltpu.make_async_copy(ref, ref, sem).wait()

    scale = (-0.5 * MORPH_FACTOR) / w_sum

    def divergence(start, count, clear):
        n = -(-count // 8)
        rows, up, dn = (pl.ds(7 + start + d, 8 * n) for d in (0, -1, 1))
        held = slice(start, start + count)
        first_lane, last_lane = wide(lane, n) == 0, wide(lane, n) == LANES - 1
        for k in range(1, blocks + 1):
            for ref in (qa, qb):
                ref[k, 24 * clear : 24 * clear + 8, :] = jnp.zeros((8, LANES), F32)

        def body(k):
            here = qb[k, rows, :]
            right = jnp.where(first_lane, qb[k + 1, rows, :], here)
            left = jnp.where(last_lane, qb[k - 1, rows, :], here)
            total = pltpu.roll(right, LANES - 1, 1) - pltpu.roll(left, 1, 1)
            total = scale * (total + (qa[k, dn, :] - qa[k, up, :]))

            def store():
                outbox[(k - 1) // share, (k - 1) % share, held] = total[0:count]

            return store

        each_block(body)
        nothing = jnp.zeros((count, LANES), F32)
        is_right = lax.broadcasted_iota(jnp.int32, (count, LANES), 1) < LANES // 2
        for to in range(nc):
            left = outbox[to - 1, share - 1, held] if to > 0 else nothing
            right = outbox[to + 1, 0, held] if to < nc - 1 else nothing
            outbox[to, share, held] = jnp.where(is_right, right, left)

    def send_edges(side):
        rows = slice(0, 3) if side == 0 else slice(EDGE - 3, EDGE)
        land, recv = (in_dn, dn_recv) if side == 0 else (in_up, up_recv)
        for d in range(nc):
            peer = lax.rem(c + d, nc)
            remote(
                outbox.at[peer, :, rows],
                land.at[d, :, 0:3],
                rs_send.at[1 + side],
                recv,
                (peer, s - 1 + 2 * side),
            )

    def send_rows(start, count):
        held = slice(start, start + count)
        for d in range(1, nc):
            peer = lax.rem(c + d, nc)
            remote(
                outbox.at[peer, :, held],
                inbox.at[d, :, held],
                rs_send.at[0],
                rs_recv,
                (peer, s),
            )

    def early_part(side):
        start = 10 if side == 0 else 0
        divergence(start, 8, 1 - side)
        send_edges(1 - side)
        send_rows(start, 8)

    def late_part(side):
        start = 0 if side == 0 else 8
        divergence(start, 10, side)
        pl.when(has(side))(lambda: send_edges(side))
        send_rows(start, 10)

    def by_slow(part):
        for value in (0, 1):
            pl.when(slow == value)(functools.partial(part, value))

    def before_side(side):
        wait_grid(side, 0)
        side_grid(side)

    def after_first_side():
        wait_grid(fast, 1, 2)
        fill_grid(grid_rim.at[fast, 1], diff, rim_rows(fast))
        pl.semaphore_wait(known.at[1], n1)
        tell(2, near + ring(4))

    first_lane3 = wide(lane, 3) == 0
    last_lane3 = wide(lane, 3) == LANES - 1

    n2, n3 = len(near) + 2, 2

    def between():
        pl.semaphore_wait(known.at[2], n2)
        tell(3, ring(8))
        wait_grid(slow, 1, 2)
        fill_grid(grid_rim.at[slow, 1], diff, rim_rows(slow), has(slow))

        def faces(k):
            rows, dn = pl.ds(7, 24), pl.ds(8, 24)

            def face(p, q):
                total = p + q
                return SLOPE_COEFF * p * q / jnp.where(total > 0.0, total, 1.0)

            d = diff[k, rows, :]
            right = jnp.where(first_lane3, diff[k + 1, rows, :], d)
            left = jnp.where(last_lane3, diff[k - 1, rows, :], d)
            f_dn = face(d, diff[k, dn, :])
            f_right = face(d, pltpu.roll(right, LANES - 1, 1))
            f_left = face(d, pltpu.roll(left, 1, 1))

            def store():
                kd[k, rows, :] = f_dn
                kr[k, rows, :] = f_right
                kl[k, rows, :] = f_left

            return store

        each_block(faces, GROUP // 4)
        def bed_block(k):
            at = pl.ds(pl.multiple_of(k * LANES, LANES), LANES)
            return (
                grid_rim[0, 2, :, at],
                grid_own[2, :, at],
                grid_rim[1, 2, :, at],
            )

        before = lax.max(share * c - 1, 0)
        after = lax.min(share * (c + 1), blocks - 1)
        beds = [bed_block(share * c + r) for r in range(share)]
        beds.append(tuple(map(beside, bed_block(before), bed_block(after))))
        for r, (above, own_rows, below) in enumerate(beds):
            slice_b[r, 0:8] = jnp.where(s > 0, above, 0.0)
            slice_b[r, 8:24] = own_rows
            slice_b[r, 24:32] = jnp.where(s < ns - 1, below, 0.0)
        for src, dst in ((kd, slice_kd), (kr, slice_kr), (kl, slice_kl)):
            for r in range(share):
                dst[r] = src[share * c + 1 + r]
            dst[share] = beside(src[share * c], src[share * (c + 1) + 1])
        by_slow(early_part)

    def side_part(i, carry):
        j, on_slow = lax.rem(i, conds), i >= conds
        side = jnp.where(on_slow, slow, fast)
        pl.when(j == 0)(lambda: before_side(side))
        wait_cond(side, j)
        side_cond(side, j)
        pl.when(i == conds - 1)(after_first_side)
        pl.when(i == 2 * conds - 2)(between)
        return carry

    lax.fori_loop(0, 2 * conds, side_part, 0)

    pl.semaphore_wait(known.at[3], n3)
    by_slow(late_part)
    landed = inbox.at[1:nc, :, 0:EDGE]
    edge_up, edge_dn = in_up.at[:, :, 0:3], in_dn.at[:, :, 0:3]
    arrive(landed, rs_recv)
    total = [outbox[c, :, 0:16], outbox[c, :, 16:EDGE]]
    for d in range(1, nc):
        total[0] = total[0] + inbox[d, :, 0:16]
        total[1] = total[1] + inbox[d, :, 16:EDGE]
    slice_b[:, 7:23] = slice_b[:, 7:23] + total[0]
    slice_b[:, 23:25] = slice_b[:, 23:25] + total[1]
    pl.when(s > 0)(lambda: arrive(edge_up, up_recv))
    pl.when(s < ns - 1)(lambda: arrive(edge_dn, dn_recv))
    for land, start in ((in_up, 6), (in_dn, 23)):
        extra = land[0, :, 0:3]
        for d in range(1, nc):
            extra = extra + land[d, :, 0:3]
        slice_b[:, start : start + 3] = slice_b[:, start : start + 3] + extra

    def image_of(get, face_dn, face_right, face_left, left, right, n):
        rows, up, dn = (slice(8 + d, 8 + d + 8 * n) for d in (0, -1, 1))
        first_lane, last_lane = wide(lane, n) == 0, wide(lane, n) == LANES - 1
        here = get(rows)
        to_right = jnp.where(first_lane, right(rows), here)
        to_left = jnp.where(last_lane, left(rows), here)
        to_dn, to_up = here - get(dn), here - get(up)
        to_right = here - pltpu.roll(to_right, LANES - 1, 1)
        to_left = here - pltpu.roll(to_left, 1, 1)
        f_dn, f_right = face_dn(rows) * to_dn, face_right(rows) * to_right
        image = f_dn + face_dn(up) * to_up + f_right + face_left(rows) * to_left
        return here, image, f_dn * to_dn + f_right * to_right

    def fold(value):
        return value[0:8] + value[8:16]

    def rows_of(ref, k):
        return lambda rows: ref[k, rows, :]

    zero = jnp.zeros((8, LANES), F32)
    bb, bl, ll, lyl = zero, zero, zero, zero
    images = []
    for r in range(share + 1):
        here, image, energy = image_of(
            rows_of(slice_b, r),
            rows_of(slice_kd, r),
            rows_of(slice_kr, r),
            rows_of(slice_kl, r),
            rows_of(slice_b, r - 1 if r else share),
            rows_of(slice_b, min(r + 1, share)),
            3,
        )
        images.append(image)
        if r < share:
            bb, bl, ll = bb + fold(here * here), bl + fold(energy), ll + fold(image * image)
    for r in range(share):
        slice_y[r] = images[r]
        here = images[r][0:16]
        right = jnp.where(wide(lane, 2) == 0, images[r + 1][0:16], here)
        to_right = here - pltpu.roll(right, LANES - 1, 1)
        to_dn = here - slice_y[r, 1:17]
        f_dn, f_right = slice_kd[r, own] * to_dn, slice_kr[r, own] * to_right
        lyl = lyl + fold(f_dn * to_dn + f_right * to_right)
    tile = zero
    for i, value in enumerate((bb, bl, ll, lyl)):
        tile = jnp.where(sub == i, jnp.sum(value, 0, keepdims=True), tile)

    half = ns // 2
    sums[0] = tile
    for e in range(2):
        for d in range(nc):
            if d or e:
                peer = (lax.rem(c + d, nc), lax.rem(s + half * e, ns))
                at = nc * e + d
                remote(sums.at[0], sums.at[at], sum_send.at[0], sum_recv.at[0], peer)
    mine = pl.ds(share * c + 1, share)
    b_own = slice_b.at[0:share, 7:25]
    for d in range(1, nc):
        peer = (lax.rem(c + d, nc), s)
        remote(b_own, b.at[mine, 7:25], ag_send, ag_recv, peer)
    b[mine, 7:23] = slice_b[0:share, 7:23]
    b[mine, 23:25] = slice_b[0:share, 23:25]

    others = sums.at[1 : 2 * nc]
    arrive(others, sum_recv.at[0])
    totals[0] = jnp.sum(sums[...], 0)
    base, place = s - lax.rem(s, half), lax.rem(s, half)
    for d in range(1, half):
        peer = (c, base + lax.rem(place + d, half))
        remote(totals.at[0], totals.at[d], sum_send.at[1], sum_recv.at[1], peer)

    gathered = b.at[1 : blocks + 1 - share, 7:25]
    arrive(gathered, ag_recv)

    def strip(k):
        _, image, _ = image_of(
            rows_of(b, k),
            rows_of(kd, k),
            rows_of(kr, k),
            rows_of(kl, k),
            rows_of(b, k - 1),
            rows_of(b, k + 1),
            2,
        )

        def store():
            y[k, 0:16] = image

        return store

    each_block(strip, GROUP // 2)
    halves = totals.at[1:half]
    arrive(halves, sum_recv.at[1])
    total = jnp.sum(jnp.sum(totals[...], 0), 1, keepdims=True)
    s_bb, s_bl, s_ll, s_lyl = (total[i : i + 1] for i in range(4))
    m1, m2, m3 = s_bl / s_bb, s_ll / s_bb, s_lyl / s_bb
    alpha0 = 1.0 / (1.0 + m1)
    beta = (m2 - m1 * m1) * alpha0 * alpha0
    p_b = m1 * alpha0 + beta
    p_l = alpha0
    pp = p_b * p_b - 2.0 * p_b * p_l * m1 + p_l * p_l * m2
    plp = p_b * p_b * m1 - 2.0 * p_b * p_l * m2 + p_l * p_l * m3
    alpha1 = beta / (pp + plp)
    x_b = alpha0 + alpha1 * p_b
    x_l = -alpha1 * p_l

    x_b, x_l = 2.0 * x_b, 2.0 * x_l
    for k in range(1, blocks + 1):
        bed_twice[:, columns(k)] = x_b * b[k, own] + x_l * y[k, 0:16]

    for side in (0, 1):

        def sent(side=side):
            of_grid, of_cond = rim_copies(side, 1 - side)
            for at in range(3):
                of_grid(at).wait_send()
            for j in range(conds):
                for copy in of_cond(j):
                    copy.wait_send()
            arrive(edge_up, rs_send.at[1 + side])

        pl.when(has(side))(sent)
    arrive(landed, rs_send.at[0])
    arrive(gathered, ag_send)
    arrive(others, sum_send.at[0])
    arrive(halves, sum_send.at[1])


def local(nc, ns, flow, forcing, wet, depth, limiter, weights, bed, diffusivity):
    conds, ny = flow.shape[0], flow.shape[-1]
    blocks = ny // LANES
    dma = pltpu.SemaphoreType.DMA

    def vmem(*shape, dtype=F32):
        return pltpu.VMEM(shape, dtype)

    def state():
        return vmem(conds * STATES, blocks + 2, TALL, LANES)

    def per_cond():
        return vmem(conds, blocks + 2, TALL, LANES)

    def grid():
        return vmem(blocks + 2, TALL, LANES)

    share = blocks // nc
    rims = 3 + 5 * conds
    any_space = pl.BlockSpec(memory_space=pl.ANY)
    in_vmem = pl.BlockSpec(memory_space=pltpu.VMEM)
    surface_twice, bed_twice = pl.pallas_call(
        functools.partial(kernel, nc, ns),
        out_shape=(
            pltpu.VMEM((conds, ROWS, ny), F32),
            pltpu.VMEM((ROWS, ny), F32),
        ),
        in_specs=[any_space] * 8,
        out_specs=(in_vmem, in_vmem),
        scratch_shapes=[
            vmem(conds, 3, ROWS, ny),
            vmem(conds, 2, ROWS, ny),
            vmem(conds, ROWS, ny, dtype=jnp.int32),
            vmem(3, ROWS, ny),
            vmem(ROWS, ny, dtype=jnp.int32),
            pltpu.SMEM((1, nc * conds), jnp.int32),
            vmem(2, conds, 3, HALO, ny),
            vmem(2, conds, 2, HALO, ny),
            vmem(2, conds, HALO, ny, dtype=jnp.int32),
            vmem(2, 3, HALO, ny),
            state(),
            state(),
            state(),
            state(),
            state(),
            per_cond(),
            per_cond(),
            per_cond(),
            grid(),
            grid(),
            grid(),
            grid(),
            vmem(nc, share + 1, 24, LANES),
            vmem(nc, share + 1, 24, LANES),
            vmem(nc, share + 1, 8, LANES),
            vmem(nc, share + 1, 8, LANES),
            grid(),
            grid(),
            grid(),
            grid(),
            grid(),
            vmem(blocks + 1, ROWS, LANES),
            vmem(share + 1, TALL + 8, LANES),
            vmem(share, 24, LANES),
            vmem(share + 1, TALL, LANES),
            vmem(share + 1, TALL, LANES),
            vmem(share + 1, TALL, LANES),
            vmem(2 * nc, 8, LANES),
            vmem(ns // 2, 8, LANES),
            dma((5 + 3 * conds,)),
            dma((2, rims)),
            dma((2, rims)),
            dma((3,)),
            dma(()),
            dma(()),
            dma(()),
            dma(()),
            dma(()),
            dma((2,)),
            dma((2,)),
            pltpu.SemaphoreType.REGULAR((4,)),
        ],
        compiler_params=pltpu.CompilerParams(
            collective_id=0, has_side_effects=True, vmem_limit_bytes=58 << 20
        ),
        cost_estimate=pl.CostEstimate(
            flops=20_000_000, bytes_accessed=4_000_000, transcendentals=0
        ),
        name="morphology",
    )(flow, forcing, wet, depth, limiter, weights.reshape(1, -1), bed, diffusivity)
    return 0.5 * surface_twice, 0.5 * bed_twice


def solution(mesh):
    in_specs = (
        P("cond", None, "space", None),
        P("cond", None, "space", None),
        P("cond", "space", None),
        P("space", None),
        P("space", None),
        P(),
        P("space", None),
        P("space", None),
    )
    out_specs = (P("cond", "space", None), P("space", None))
    body = functools.partial(local, mesh.shape["cond"], mesh.shape["space"])
    return jax.shard_map(body, mesh=mesh, in_specs=in_specs, out_specs=out_specs, check_vma=False)
```

```python
import functools

import jax
import jax.numpy as jnp
from jax import lax
from jax.experimental import pallas as pl
from jax.experimental.pallas import tpu as pltpu
from jax.sharding import PartitionSpec as P

MESH = pl.DeviceIdType.MESH
F32 = jnp.float32

STEPS = 4
TIME_STEP = 0.4
GRAVITY = 1.0
FRICTION = 0.1
TRANSPORT_BASE = 0.5
MORPH_FACTOR = 1.0
SLOPE_COEFF = 1.0

LANES = 128
ROWS = 16
HALO = 8
TALL = ROWS + 2 * HALO
HALF_STEPS = 2 * STEPS
STATES = HALF_STEPS + 1
EDGE = 18
GROUP = 8


def kernel(
    nc,
    ns,
    flow,
    forcing,
    wet,
    depth,
    limiter,
    weights,
    bed,
    diffusivity,
    surface_twice,
    bed_twice,
    flow_own,
    force_own,
    wet_own,
    grid_own,
    lim_own,
    w_own,
    flow_rim,
    force_rim,
    wet_rim,
    grid_rim,
    eta,
    vel_a,
    vel_b,
    dva,
    dvb,
    mask,
    fa,
    fb,
    dep,
    lim,
    qa,
    qb,
    outbox,
    inbox,
    in_up,
    in_dn,
    diff,
    kd,
    kr,
    kl,
    b,
    y,
    slice_b,
    slice_y,
    slice_kd,
    slice_kr,
    slice_kl,
    sums,
    totals,
    load_sem,
    rim_send,
    rim_recv,
    rs_send,
    rs_recv,
    up_recv,
    dn_recv,
    ag_send,
    ag_recv,
    sum_send,
    sum_recv,
    known,
):
    c = lax.axis_index("cond")
    s = lax.axis_index("space")
    blocks = kd.shape[0] - 2
    conds = flow.shape[0]
    share = blocks // nc
    lane = lax.broadcasted_iota(jnp.int32, (8, LANES), 1)
    sub = lax.broadcasted_iota(jnp.int32, (8, LANES), 0)

    def wide(pattern, n):
        return pattern if n == 1 else jnp.concatenate([pattern] * n, 0)

    def each_block(body, size=GROUP):
        for at in range(1, blocks + 1, size):
            for store in [body(k) for k in range(at, at + size)]:
                store()

    for ref in (in_up, in_dn):
        ref[:, :, 0:3] = jnp.zeros((nc, share + 1, 3, LANES), F32)

    near_space = [(c, lax.rem(s + d, ns)) for d in (1, ns - 1)]
    near_cond = [(c + 1 - 2 * lax.rem(c, 2), s)]
    near_cond += [(lax.rem(c + d, nc), s) for d in (2, nc - 2)]
    near = near_space + near_cond
    barrier = pltpu.get_barrier_semaphore()
    for peer in near:
        pl.semaphore_signal(barrier, inc=1, device_id=peer, device_id_type=MESH)

    pl.semaphore_wait(barrier, len(near))

    slow = lax.rem(s, 2)
    fast = 1 - slow

    def has(side):
        return jnp.where(side == 0, s > 0, s < ns - 1)

    def rim_copies(side, slot):
        peer = (c, s - 1 + 2 * side)

        def rows(count):
            if side == 0:
                return slice(0, count), slice(0, count)
            return slice(ROWS - count, ROWS), slice(HALO - count, HALO)

        def grid_pair(src, at, count):
            here, there = rows(count)
            return src.at[here], grid_rim.at[slot, at, there]

        def cond_pair(src, dst, count, *index):
            here, there = rows(count)
            return src.at[(*index, here)], dst.at[(slot, *index, there)]

        def copy(i, pair):
            return pltpu.make_async_remote_copy(
                *pair,
                rim_send.at[side, i],
                rim_recv.at[slot, i],
                device_id=peer,
                device_id_type=MESH,
            )

        def of_grid(at):
            src, count = ((depth, HALO), (diffusivity, 2), (bed, 2))[at]
            return copy(at, grid_pair(src, at, count))

        def of_cond(j):
            here, there = rows(HALO)
            pairs = [
                (flow.at[j, 0:2, here], flow_rim.at[slot, j, 0:2, there]),
                cond_pair(flow, flow_rim, HALO - 1, j, 2),
                cond_pair(forcing, force_rim, HALO - 1, j, 0),
                cond_pair(forcing, force_rim, HALO - 2, j, 1),
                cond_pair(wet, wet_rim, HALO - 1, j),
            ]
            return [copy(3 + 5 * j + i, pair) for i, pair in enumerate(pairs)]

        return of_grid, of_cond

    def start_rims(side):
        of_grid, of_cond = rim_copies(side, 1 - side)
        of_grid(0).start()
        for copy in of_cond(0):
            copy.start()
        of_grid(1).start()
        of_grid(2).start()
        for j in range(1, conds):
            for copy in of_cond(j):
                copy.start()

    def by_side(side, body):
        for value in (0, 1):
            real = jnp.logical_and(side == value, has(value))
            pl.when(real)(functools.partial(body, *rim_copies(value, value)))

    def wait_grid(side, *which):
        def wait(of_grid, of_cond):
            for at in which:
                of_grid(at).wait_recv()

        by_side(side, wait)

    def wait_cond(side, j):
        def wait(of_grid, of_cond):
            for copy in of_cond(j):
                copy.wait_recv()

        by_side(side, wait)

    for order in (0, 1):
        for side in (order, 1 - order):
            go = jnp.logical_and(slow == order, has(side))
            pl.when(go)(functools.partial(start_rims, side))

    def loads_grid():
        pairs = [
            (depth, grid_own.at[0]),
            (weights, w_own),
            (limiter, lim_own),
            (diffusivity, grid_own.at[1]),
            (bed, grid_own.at[2]),
        ]
        return [
            pltpu.make_async_copy(src, dst, load_sem.at[i])
            for i, (src, dst) in enumerate(pairs)
        ]

    def loads_cond(j):
        pairs = [
            (flow.at[j], flow_own.at[j]),
            (forcing.at[j], force_own.at[j]),
            (wet.at[j], wet_own.at[j]),
        ]
        return [
            pltpu.make_async_copy(src, dst, load_sem.at[5 + 3 * j + i])
            for i, (src, dst) in enumerate(pairs)
        ]

    l_depth, l_w, l_lim, l_diff, l_bed = loads_grid()
    for copy in [l_depth, l_w, l_lim] + loads_cond(0):
        copy.start()
    for j in range(1, conds):
        for copy in loads_cond(j):
            copy.start()
    l_diff.start()
    l_bed.start()

    for ref in (eta, dvb):
        for block in (0, blocks + 1):
            ref[:, block] = jnp.zeros((conds * STATES, TALL, LANES), F32)
    for ref in (qb, diff, b, kd, kr, kl):
        for block in (0, blocks + 1):
            ref[block] = jnp.zeros(ref.shape[1:], F32)
    for block in range(1, blocks + 1):
        qa[block] = jnp.zeros((TALL, LANES), F32)
        qb[block] = jnp.zeros((TALL, LANES), F32)

    def tell(step, peers):
        for peer in peers:
            pl.semaphore_signal(
                known.at[step], inc=1, device_id=peer, device_id_type=MESH
            )
        return len(peers)

    def ring(d):
        return [(c, lax.rem(s + d, ns)), (c, lax.rem(s + ns - d, ns))]

    n0 = tell(0, near)

    def columns(k):
        return slice((k - 1) * LANES, k * LANES)

    def fill_grid(src, dst, rows, real=None):
        def body(k):
            value = src[:, columns(k)]
            if real is not None:
                value = jnp.where(real, value, jnp.zeros_like(value))

            def store():
                dst[k, rows, :] = value

            return store

        each_block(body)

    def fill_cond(j, flow_src, force_src, wet_src, rows, real=None):
        at0 = j * STATES

        def body(k):
            at = columns(k)

            def get(value):
                if real is None:
                    return value
                return jnp.where(real, value, jnp.zeros_like(value))

            d = dep[k, rows, :]
            e = get(flow_src[0, :, at])
            u = get(flow_src[1, :, at])
            v = get(flow_src[2, :, at])
            m = get(wet_src[:, at]).astype(F32) * (0.5 * TIME_STEP)
            force_a = 2.0 * m * get(force_src[0, :, at])
            force_b = 2.0 * m * get(force_src[1, :, at])

            def store():
                eta[at0, k, rows, :] = e
                vel_a[at0, k, rows, :] = u
                vel_b[at0, k, rows, :] = v
                dva[at0, k, rows, :] = d * u
                dvb[at0, k, rows, :] = d * v
                mask[j, k, rows, :] = m
                fa[j, k, rows, :] = force_a
                fb[j, k, rows, :] = force_b

            return store

        each_block(body, GROUP // 2)

    own = pl.ds(HALO, ROWS)
    l_depth.wait()
    fill_grid(grid_own.at[0], dep, own)

    def advance(j, t, k, start, n):
        at = j * STATES + t
        first_lane, last_lane = wide(lane, n) == 0, wide(lane, n) == LANES - 1
        rows, up, dn = (pl.ds(start + d, 8 * n) for d in (0, -1, 1))

        def across(ref):
            here = ref[at, k, rows, :]
            right = jnp.where(first_lane, ref[at, k + 1, rows, :], here)
            left = jnp.where(last_lane, ref[at, k - 1, rows, :], here)
            return here, pltpu.roll(right, LANES - 1, 1) - pltpu.roll(left, 1, 1)

        e, e_across = across(eta)
        _, h_across = across(dvb)
        m = mask[j, k, rows, :]
        keep = 1.0 - (2.0 * FRICTION) * m
        e_next = e - m * (dva[at, k, dn, :] - dva[at, k, up, :] + h_across)
        slope = GRAVITY * m
        u_next = keep * vel_a[at, k, rows, :] + fa[j, k, rows, :]
        u_next = u_next - slope * (eta[at, k, dn, :] - eta[at, k, up, :])
        v_next = keep * vel_b[at, k, rows, :] + fb[j, k, rows, :] - slope * e_across
        return e_next, u_next, v_next

    def put(j, t, k, start, n, state):
        at = j * STATES + t
        rows = pl.ds(start, 8 * n)
        e, u, v = state
        d = dep[k, rows, :]
        eta[at, k, rows, :] = e
        vel_a[at, k, rows, :] = u
        vel_b[at, k, rows, :] = v
        dva[at, k, rows, :] = d * u
        dvb[at, k, rows, :] = d * v

    def first(j, t, start, n):
        def body(k):
            state = advance(j, t - 1, k, start, n)
            return lambda: put(j, t, k, start, n, state)

        each_block(body, GROUP // n)

    def second(j, t, start, n, weight, valid=None):
        def body(k):
            at = j * STATES + t - 2
            rows = pl.ds(start, 8 * n)
            e, u, v = advance(j, t - 1, k, start, n)
            e = 0.5 * (eta[at, k, rows, :] + e)
            u = 0.5 * (vel_a[at, k, rows, :] + u)
            v = 0.5 * (vel_b[at, k, rows, :] + v)
            energy = u * u + v * v
            factor = weight * (TRANSPORT_BASE + energy)
            factor = factor / (1.0 + lim[k, rows, :] * energy)
            add_a, add_b = u * factor, v * factor
            if valid is not None:
                add_a = jnp.where(valid, add_a, 0.0)
                add_b = jnp.where(valid, add_b, 0.0)
            sum_a = qa[k, rows, :] + add_a
            sum_b = qb[k, rows, :] + add_b

            def store():
                put(j, t, k, start, n, (e, u, v))
                qa[k, rows, :] = sum_a
                qb[k, rows, :] = sum_b

            return store

        each_block(body, GROUP // n)

    def interior(j, weight):
        def pair(p, carry, n):
            t = 2 * p + 1
            first(j, t, HALO + t, n)
            place = jnp.concatenate([sub + 8 * i for i in range(n)], 0)
            second(j, t + 1, HALO + t + 1, n, weight, place < ROWS - 2 * (t + 1))
            return carry

        lax.fori_loop(0, 2, functools.partial(pair, n=2), 0)
        for p in range(2, STEPS - 1):
            pair(p, 0, 1)
        first(j, HALF_STEPS - 1, HALO + HALF_STEPS - 1, 1)

    def side_steps(j, side, weight):
        def pair(p, carry):
            t = 2 * p + 1
            first(j, t, jnp.where(side == 0, t, 24 - t), 1)
            t = 2 * p + 2
            second(j, t, jnp.where(side == 0, t, 24 - t), 1, weight)
            return carry

        lax.fori_loop(0, STEPS, pair, 0)
        rows = pl.ds(pl.multiple_of(8 * side, 8), 8)
        held = pl.ds(pl.multiple_of(8 + 8 * side, 8), 8)
        for k in range(1, blocks + 1):
            state = eta[j * STATES + HALF_STEPS, k, held, :]
            surface_twice[j, rows, columns(k)] = 2.0 * state

    l_w.wait()
    w_sum = w_own[0, 0]
    for i in range(1, nc * conds):
        w_sum = w_sum + w_own[0, i]
    w_sum = w_sum.astype(F32)

    def lim_rows():
        l_lim.wait()

        def body(k):
            value = lim_own[:, columns(k)].astype(F32)

            def store():
                lim[k, own, :] = value
                lim[k, 0:8, :] = jnp.zeros((8, LANES), F32)
                lim[k, 24:32, :] = jnp.zeros((8, LANES), F32)

            return store

        each_block(body)

    lim_rows()
    def weight_of(j):
        return w_own[0, conds * c + j].astype(F32)

    def start_cond(j, carry):
        for copy in loads_cond(j):
            copy.wait()
        fill_cond(j, flow_own.at[j], force_own.at[j], wet_own.at[j], own)
        interior(j, weight_of(j))
        return carry

    lax.fori_loop(0, conds, start_cond, 0)
    pl.semaphore_wait(known.at[0], n0)
    n1 = tell(1, near + ring(2))
    l_diff.wait()
    l_bed.wait()
    fill_grid(grid_own.at[1], diff, own)

    def rim_rows(side):
        return pl.ds(pl.multiple_of(24 * side, 8), 8)

    def side_grid(side):
        fill_grid(grid_rim.at[side, 0], dep, rim_rows(side), has(side))

    def side_cond(side, j):
        fill_cond(
            j,
            flow_rim.at[side, j],
            force_rim.at[side, j],
            wet_rim.at[side, j],
            rim_rows(side),
            has(side),
        )
        side_steps(j, side, weight_of(j))

    right_part = lane < LANES // 2

    def beside(left, right):
        return jnp.where(wide(right_part, left.shape[0] // 8), right, left)

    def remote(src, dst, send, recv, peer):
        copy = pltpu.make_async_remote_copy(
            src, dst, send, recv, device_id=peer, device_id_type=MESH
        )
        copy.start()

    def arrive(ref, sem):
        pltpu.make_async_copy(ref, ref, sem).wait()

    scale = (-0.5 * MORPH_FACTOR) / w_sum

    def divergence(start, count, clear):
        n = -(-count // 8)
        rows, up, dn = (pl.ds(7 + start + d, 8 * n) for d in (0, -1, 1))
        held = slice(start, start + count)
        first_lane, last_lane = wide(lane, n) == 0, wide(lane, n) == LANES - 1
        for k in range(1, blocks + 1):
            for ref in (qa, qb):
                ref[k, 24 * clear : 24 * clear + 8, :] = jnp.zeros((8, LANES), F32)

        def body(k):
            here = qb[k, rows, :]
            right = jnp.where(first_lane, qb[k + 1, rows, :], here)
            left = jnp.where(last_lane, qb[k - 1, rows, :], here)
            total = pltpu.roll(right, LANES - 1, 1) - pltpu.roll(left, 1, 1)
            total = scale * (total + (qa[k, dn, :] - qa[k, up, :]))

            def store():
                outbox[(k - 1) // share, (k - 1) % share, held] = total[0:count]

            return store

        each_block(body)
        nothing = jnp.zeros((count, LANES), F32)
        is_right = lax.broadcasted_iota(jnp.int32, (count, LANES), 1) < LANES // 2
        for to in range(nc):
            left = outbox[to - 1, share - 1, held] if to > 0 else nothing
            right = outbox[to + 1, 0, held] if to < nc - 1 else nothing
            outbox[to, share, held] = jnp.where(is_right, right, left)

    def send_edges(side):
        rows = slice(0, 3) if side == 0 else slice(EDGE - 3, EDGE)
        land, recv = (in_dn, dn_recv) if side == 0 else (in_up, up_recv)
        for d in range(nc):
            peer = lax.rem(c + d, nc)
            remote(
                outbox.at[peer, :, rows],
                land.at[d, :, 0:3],
                rs_send.at[1 + side],
                recv,
                (peer, s - 1 + 2 * side),
            )

    def send_rows(start, count):
        held = slice(start, start + count)
        for d in range(1, nc):
            peer = lax.rem(c + d, nc)
            remote(
                outbox.at[peer, :, held],
                inbox.at[d, :, held],
                rs_send.at[0],
                rs_recv,
                (peer, s),
            )

    def early_part(side):
        start = 10 if side == 0 else 0
        divergence(start, 8, 1 - side)
        send_edges(1 - side)
        send_rows(start, 8)

    def late_part(side):
        start = 0 if side == 0 else 8
        divergence(start, 10, side)
        pl.when(has(side))(lambda: send_edges(side))
        send_rows(start, 10)

    def by_slow(part):
        for value in (0, 1):
            pl.when(slow == value)(functools.partial(part, value))

    def before_side(side):
        wait_grid(side, 0)
        side_grid(side)

    def after_first_side():
        wait_grid(fast, 1, 2)
        fill_grid(grid_rim.at[fast, 1], diff, rim_rows(fast))
        pl.semaphore_wait(known.at[1], n1)
        tell(2, near + ring(4))

    first_lane3 = wide(lane, 3) == 0
    last_lane3 = wide(lane, 3) == LANES - 1

    n2, n3 = len(near) + 2, 2

    def between():
        pl.semaphore_wait(known.at[2], n2)
        tell(3, ring(8))
        wait_grid(slow, 1, 2)
        fill_grid(grid_rim.at[slow, 1], diff, rim_rows(slow), has(slow))

        def faces(k):
            rows, dn = pl.ds(7, 24), pl.ds(8, 24)

            def face(p, q):
                total = p + q
                return SLOPE_COEFF * p * q / jnp.where(total > 0.0, total, 1.0)

            d = diff[k, rows, :]
            right = jnp.where(first_lane3, diff[k + 1, rows, :], d)
            left = jnp.where(last_lane3, diff[k - 1, rows, :], d)
            f_dn = face(d, diff[k, dn, :])
            f_right = face(d, pltpu.roll(right, LANES - 1, 1))
            f_left = face(d, pltpu.roll(left, 1, 1))

            def store():
                kd[k, rows, :] = f_dn
                kr[k, rows, :] = f_right
                kl[k, rows, :] = f_left

            return store

        each_block(faces, GROUP // 4)
        def bed_block(k):
            at = pl.ds(pl.multiple_of(k * LANES, LANES), LANES)
            return (
                grid_rim[0, 2, :, at],
                grid_own[2, :, at],
                grid_rim[1, 2, :, at],
            )

        before = lax.max(share * c - 1, 0)
        after = lax.min(share * (c + 1), blocks - 1)
        beds = [bed_block(share * c + r) for r in range(share)]
        beds.append(tuple(map(beside, bed_block(before), bed_block(after))))
        for r, (above, own_rows, below) in enumerate(beds):
            slice_b[r, 0:8] = jnp.where(s > 0, above, 0.0)
            slice_b[r, 8:24] = own_rows
            slice_b[r, 24:32] = jnp.where(s < ns - 1, below, 0.0)
        for src, dst in ((kd, slice_kd), (kr, slice_kr), (kl, slice_kl)):
            for r in range(share):
                dst[r] = src[share * c + 1 + r]
            dst[share] = beside(src[share * c], src[share * (c + 1) + 1])
        by_slow(early_part)

    def side_part(i, carry):
        j, on_slow = lax.rem(i, conds), i >= conds
        side = jnp.where(on_slow, slow, fast)
        pl.when(j == 0)(lambda: before_side(side))
        wait_cond(side, j)
        side_cond(side, j)
        pl.when(i == conds - 1)(after_first_side)
        pl.when(i == 2 * conds - 2)(between)
        return carry

    lax.fori_loop(0, 2 * conds, side_part, 0)

    pl.semaphore_wait(known.at[3], n3)
    by_slow(late_part)
    landed = inbox.at[1:nc, :, 0:EDGE]
    edge_up, edge_dn = in_up.at[:, :, 0:3], in_dn.at[:, :, 0:3]
    arrive(landed, rs_recv)
    total = [outbox[c, :, 0:16], outbox[c, :, 16:EDGE]]
    for d in range(1, nc):
        total[0] = total[0] + inbox[d, :, 0:16]
        total[1] = total[1] + inbox[d, :, 16:EDGE]
    slice_b[:, 7:23] = slice_b[:, 7:23] + total[0]
    slice_b[:, 23:25] = slice_b[:, 23:25] + total[1]
    pl.when(s > 0)(lambda: arrive(edge_up, up_recv))
    pl.when(s < ns - 1)(lambda: arrive(edge_dn, dn_recv))
    for land, start in ((in_up, 6), (in_dn, 23)):
        extra = land[0, :, 0:3]
        for d in range(1, nc):
            extra = extra + land[d, :, 0:3]
        slice_b[:, start : start + 3] = slice_b[:, start : start + 3] + extra

    def image_of(get, face_dn, face_right, face_left, left, right, n):
        rows, up, dn = (slice(8 + d, 8 + d + 8 * n) for d in (0, -1, 1))
        first_lane, last_lane = wide(lane, n) == 0, wide(lane, n) == LANES - 1
        here = get(rows)
        to_right = jnp.where(first_lane, right(rows), here)
        to_left = jnp.where(last_lane, left(rows), here)
        to_dn, to_up = here - get(dn), here - get(up)
        to_right = here - pltpu.roll(to_right, LANES - 1, 1)
        to_left = here - pltpu.roll(to_left, 1, 1)
        f_dn, f_right = face_dn(rows) * to_dn, face_right(rows) * to_right
        image = f_dn + face_dn(up) * to_up + f_right + face_left(rows) * to_left
        return here, image, f_dn * to_dn + f_right * to_right

    def fold(value):
        return value[0:8] + value[8:16]

    def rows_of(ref, k):
        return lambda rows: ref[k, rows, :]

    zero = jnp.zeros((8, LANES), F32)
    bb, bl, ll, lyl = zero, zero, zero, zero
    images = []
    for r in range(share + 1):
        here, image, energy = image_of(
            rows_of(slice_b, r),
            rows_of(slice_kd, r),
            rows_of(slice_kr, r),
            rows_of(slice_kl, r),
            rows_of(slice_b, r - 1 if r else share),
            rows_of(slice_b, min(r + 1, share)),
            3,
        )
        images.append(image)
        if r < share:
            bb, bl, ll = bb + fold(here * here), bl + fold(energy), ll + fold(image * image)
    for r in range(share):
        slice_y[r] = images[r]
        here = images[r][0:16]
        right = jnp.where(wide(lane, 2) == 0, images[r + 1][0:16], here)
        to_right = here - pltpu.roll(right, LANES - 1, 1)
        to_dn = here - slice_y[r, 1:17]
        f_dn, f_right = slice_kd[r, own] * to_dn, slice_kr[r, own] * to_right
        lyl = lyl + fold(f_dn * to_dn + f_right * to_right)
    tile = zero
    for i, value in enumerate((bb, bl, ll, lyl)):
        tile = jnp.where(sub == i, jnp.sum(value, 0, keepdims=True), tile)

    half = ns // 2
    sums[0] = tile
    for e in range(2):
        for d in range(nc):
            if d or e:
                peer = (lax.rem(c + d, nc), lax.rem(s + half * e, ns))
                at = nc * e + d
                remote(sums.at[0], sums.at[at], sum_send.at[0], sum_recv.at[0], peer)
    mine = pl.ds(share * c + 1, share)
    b[mine, 7:23] = slice_b[0:share, 7:23]
    b[mine, 23:25] = slice_b[0:share, 23:25]

    others = sums.at[1 : 2 * nc]
    arrive(others, sum_recv.at[0])
    totals[0] = jnp.sum(sums[...], 0)
    base, place = s - lax.rem(s, half), lax.rem(s, half)
    for d in range(1, half):
        peer = (c, base + lax.rem(place + d, half))
        remote(totals.at[0], totals.at[d], sum_send.at[1], sum_recv.at[1], peer)

    b_own = slice_b.at[0:share, 7:25]
    for d in range(1, nc):
        peer = (lax.rem(c + d, nc), s)
        remote(b_own, b.at[mine, 7:25], ag_send, ag_recv, peer)

    gathered = b.at[1 : blocks + 1 - share, 7:25]
    arrive(gathered, ag_recv)

    def strip(k):
        _, image, _ = image_of(
            rows_of(b, k),
            rows_of(kd, k),
            rows_of(kr, k),
            rows_of(kl, k),
            rows_of(b, k - 1),
            rows_of(b, k + 1),
            2,
        )

        def store():
            y[k, 0:16] = image

        return store

    each_block(strip, GROUP // 2)
    halves = totals.at[1:half]
    for side in (0, 1):

        def sent(side=side):
            of_grid, of_cond = rim_copies(side, 1 - side)
            for at in range(3):
                of_grid(at).wait_send()
            for j in range(conds):
                for copy in of_cond(j):
                    copy.wait_send()
            arrive(edge_up, rs_send.at[1 + side])

        pl.when(has(side))(sent)
    arrive(landed, rs_send.at[0])
    arrive(gathered, ag_send)
    arrive(others, sum_send.at[0])
    arrive(halves, sum_send.at[1])

    arrive(halves, sum_recv.at[1])
    total = jnp.sum(jnp.sum(totals[...], 0), 1, keepdims=True)
    s_bb, s_bl, s_ll, s_lyl = (total[i : i + 1] for i in range(4))
    m1, m2, m3 = s_bl / s_bb, s_ll / s_bb, s_lyl / s_bb
    alpha0 = 1.0 / (1.0 + m1)
    beta = (m2 - m1 * m1) * alpha0 * alpha0
    p_b = m1 * alpha0 + beta
    p_l = alpha0
    pp = p_b * p_b - 2.0 * p_b * p_l * m1 + p_l * p_l * m2
    plp = p_b * p_b * m1 - 2.0 * p_b * p_l * m2 + p_l * p_l * m3
    alpha1 = beta / (pp + plp)
    x_b = alpha0 + alpha1 * p_b
    x_l = -alpha1 * p_l

    x_b, x_l = 2.0 * x_b, 2.0 * x_l
    for k in range(1, blocks + 1):
        bed_twice[:, columns(k)] = x_b * b[k, own] + x_l * y[k, 0:16]


def local(nc, ns, flow, forcing, wet, depth, limiter, weights, bed, diffusivity):
    conds, ny = flow.shape[0], flow.shape[-1]
    blocks = ny // LANES
    dma = pltpu.SemaphoreType.DMA

    def vmem(*shape, dtype=F32):
        return pltpu.VMEM(shape, dtype)

    def state():
        return vmem(conds * STATES, blocks + 2, TALL, LANES)

    def per_cond():
        return vmem(conds, blocks + 2, TALL, LANES)

    def grid():
        return vmem(blocks + 2, TALL, LANES)

    share = blocks // nc
    rims = 3 + 5 * conds
    any_space = pl.BlockSpec(memory_space=pl.ANY)
    in_vmem = pl.BlockSpec(memory_space=pltpu.VMEM)
    surface_twice, bed_twice = pl.pallas_call(
        functools.partial(kernel, nc, ns),
        out_shape=(
            pltpu.VMEM((conds, ROWS, ny), F32),
            pltpu.VMEM((ROWS, ny), F32),
        ),
        in_specs=[any_space] * 8,
        out_specs=(in_vmem, in_vmem),
        scratch_shapes=[
            vmem(conds, 3, ROWS, ny),
            vmem(conds, 2, ROWS, ny),
            vmem(conds, ROWS, ny, dtype=jnp.int32),
            vmem(3, ROWS, ny),
            vmem(ROWS, ny, dtype=jnp.int32),
            pltpu.SMEM((1, nc * conds), jnp.int32),
            vmem(2, conds, 3, HALO, ny),
            vmem(2, conds, 2, HALO, ny),
            vmem(2, conds, HALO, ny, dtype=jnp.int32),
            vmem(2, 3, HALO, ny),
            state(),
            state(),
            state(),
            state(),
            state(),
            per_cond(),
            per_cond(),
            per_cond(),
            grid(),
            grid(),
            grid(),
            grid(),
            vmem(nc, share + 1, 24, LANES),
            vmem(nc, share + 1, 24, LANES),
            vmem(nc, share + 1, 8, LANES),
            vmem(nc, share + 1, 8, LANES),
            grid(),
            grid(),
            grid(),
            grid(),
            grid(),
            vmem(blocks + 1, ROWS, LANES),
            vmem(share + 1, TALL + 8, LANES),
            vmem(share, 24, LANES),
            vmem(share + 1, TALL, LANES),
            vmem(share + 1, TALL, LANES),
            vmem(share + 1, TALL, LANES),
            vmem(2 * nc, 8, LANES),
            vmem(ns // 2, 8, LANES),
            dma((5 + 3 * conds,)),
            dma((2, rims)),
            dma((2, rims)),
            dma((3,)),
            dma(()),
            dma(()),
            dma(()),
            dma(()),
            dma(()),
            dma((2,)),
            dma((2,)),
            pltpu.SemaphoreType.REGULAR((4,)),
        ],
        compiler_params=pltpu.CompilerParams(
            collective_id=0, has_side_effects=True, vmem_limit_bytes=58 << 20
        ),
        cost_estimate=pl.CostEstimate(
            flops=20_000_000, bytes_accessed=4_000_000, transcendentals=0
        ),
        name="morphology",
    )(flow, forcing, wet, depth, limiter, weights.reshape(1, -1), bed, diffusivity)
    return 0.5 * surface_twice, 0.5 * bed_twice


def solution(mesh):
    in_specs = (
        P("cond", None, "space", None),
        P("cond", None, "space", None),
        P("cond", "space", None),
        P("space", None),
        P("space", None),
        P(),
        P("space", None),
        P("space", None),
    )
    out_specs = (P("cond", "space", None), P("space", None))
    body = functools.partial(local, mesh.shape["cond"], mesh.shape["space"])
    return jax.shard_map(body, mesh=mesh, in_specs=in_specs, out_specs=out_specs, check_vma=False)
```

```python
import functools

import jax
import jax.numpy as jnp
from jax import lax
from jax.experimental import pallas as pl
from jax.experimental.pallas import tpu as pltpu
from jax.sharding import PartitionSpec as P

MESH = pl.DeviceIdType.MESH
F32 = jnp.float32

STEPS = 4
TIME_STEP = 0.4
GRAVITY = 1.0
FRICTION = 0.1
TRANSPORT_BASE = 0.5
MORPH_FACTOR = 1.0
SLOPE_COEFF = 1.0

LANES = 128
ROWS = 16
HALO = 8
TALL = ROWS + 2 * HALO
HALF_STEPS = 2 * STEPS
STATES = HALF_STEPS + 1
EDGE = 18
GROUP = 8


def kernel(
    nc,
    ns,
    flow,
    forcing,
    wet,
    depth,
    limiter,
    weights,
    bed,
    diffusivity,
    surface_twice,
    bed_twice,
    flow_own,
    force_own,
    wet_own,
    grid_own,
    lim_own,
    w_own,
    flow_rim,
    force_rim,
    wet_rim,
    grid_rim,
    eta,
    vel_a,
    vel_b,
    dva,
    dvb,
    mask,
    fa,
    fb,
    dep,
    lim,
    qa,
    qb,
    outbox,
    inbox,
    in_up,
    in_dn,
    diff,
    kd,
    kr,
    kl,
    b,
    y,
    slice_b,
    slice_y,
    slice_kd,
    slice_kr,
    slice_kl,
    sums,
    totals,
    load_sem,
    rim_send,
    rim_recv,
    rs_send,
    rs_recv,
    up_recv,
    dn_recv,
    ag_send,
    ag_recv,
    sum_send,
    sum_recv,
    known,
):
    c = lax.axis_index("cond")
    s = lax.axis_index("space")
    blocks = kd.shape[0] - 2
    conds = flow.shape[0]
    share = blocks // nc
    lane = lax.broadcasted_iota(jnp.int32, (8, LANES), 1)
    sub = lax.broadcasted_iota(jnp.int32, (8, LANES), 0)

    def wide(pattern, n):
        return pattern if n == 1 else jnp.concatenate([pattern] * n, 0)

    def each_block(body, size=GROUP):
        for at in range(1, blocks + 1, size):
            for store in [body(k) for k in range(at, at + size)]:
                store()

    for ref in (in_up, in_dn):
        ref[:, :, 0:3] = jnp.zeros((nc, share + 1, 3, LANES), F32)

    near_space = [(c, lax.rem(s + d, ns)) for d in (1, ns - 1)]
    near_cond = [(c + 1 - 2 * lax.rem(c, 2), s)]
    near_cond += [(lax.rem(c + d, nc), s) for d in (2, nc - 2)]
    near = near_space + near_cond
    barrier = pltpu.get_barrier_semaphore()
    for peer in near:
        pl.semaphore_signal(barrier, inc=1, device_id=peer, device_id_type=MESH)

    pl.semaphore_wait(barrier, len(near))

    slow = lax.rem(s, 2)
    fast = 1 - slow

    def has(side):
        return jnp.where(side == 0, s > 0, s < ns - 1)

    def rim_copies(side, slot):
        peer = (c, s - 1 + 2 * side)

        def rows(count):
            if side == 0:
                return slice(0, count), slice(0, count)
            return slice(ROWS - count, ROWS), slice(HALO - count, HALO)

        def grid_pair(src, at, count):
            here, there = rows(count)
            return src.at[here], grid_rim.at[slot, at, there]

        def cond_pair(src, dst, count, *index):
            here, there = rows(count)
            return src.at[(*index, here)], dst.at[(slot, *index, there)]

        def copy(i, pair):
            return pltpu.make_async_remote_copy(
                *pair,
                rim_send.at[side, i],
                rim_recv.at[slot, i],
                device_id=peer,
                device_id_type=MESH,
            )

        def of_grid(at):
            src, count = ((depth, HALO), (diffusivity, 2), (bed, 2))[at]
            return copy(at, grid_pair(src, at, count))

        def of_cond(j):
            here, there = rows(HALO)
            pairs = [
                (flow.at[j, 0:2, here], flow_rim.at[slot, j, 0:2, there]),
                cond_pair(flow, flow_rim, HALO - 1, j, 2),
                cond_pair(forcing, force_rim, HALO - 1, j, 0),
                cond_pair(forcing, force_rim, HALO - 2, j, 1),
                cond_pair(wet, wet_rim, HALO - 1, j),
            ]
            return [copy(3 + 5 * j + i, pair) for i, pair in enumerate(pairs)]

        return of_grid, of_cond

    def start_rims(side):
        of_grid, of_cond = rim_copies(side, 1 - side)
        of_grid(0).start()
        for copy in of_cond(0):
            copy.start()
        for j in range(1, conds):
            for copy in of_cond(j):
                copy.start()
        of_grid(1).start()
        of_grid(2).start()

    def by_side(side, body):
        for value in (0, 1):
            real = jnp.logical_and(side == value, has(value))
            pl.when(real)(functools.partial(body, *rim_copies(value, value)))

    def wait_grid(side, *which):
        def wait(of_grid, of_cond):
            for at in which:
                of_grid(at).wait_recv()

        by_side(side, wait)

    def wait_cond(side, j):
        def wait(of_grid, of_cond):
            for copy in of_cond(j):
                copy.wait_recv()

        by_side(side, wait)

    for order in (0, 1):
        for side in (order, 1 - order):
            go = jnp.logical_and(slow == order, has(side))
            pl.when(go)(functools.partial(start_rims, side))

    def loads_grid():
        pairs = [
            (depth, grid_own.at[0]),
            (weights, w_own),
            (limiter, lim_own),
            (diffusivity, grid_own.at[1]),
            (bed, grid_own.at[2]),
        ]
        return [
            pltpu.make_async_copy(src, dst, load_sem.at[i])
            for i, (src, dst) in enumerate(pairs)
        ]

    def loads_cond(j):
        pairs = [
            (flow.at[j], flow_own.at[j]),
            (forcing.at[j], force_own.at[j]),
            (wet.at[j], wet_own.at[j]),
        ]
        return [
            pltpu.make_async_copy(src, dst, load_sem.at[5 + 3 * j + i])
            for i, (src, dst) in enumerate(pairs)
        ]

    l_depth, l_w, l_lim, l_diff, l_bed = loads_grid()
    for copy in [l_depth, l_w, l_lim] + loads_cond(0):
        copy.start()
    for j in range(1, conds):
        for copy in loads_cond(j):
            copy.start()
    l_diff.start()
    l_bed.start()

    for ref in (eta, dvb):
        for block in (0, blocks + 1):
            ref[:, block] = jnp.zeros((conds * STATES, TALL, LANES), F32)
    for ref in (qb, diff, b, kd, kr, kl):
        for block in (0, blocks + 1):
            ref[block] = jnp.zeros(ref.shape[1:], F32)
    for block in range(1, blocks + 1):
        qa[block] = jnp.zeros((TALL, LANES), F32)
        qb[block] = jnp.zeros((TALL, LANES), F32)

    def tell(step, peers):
        for peer in peers:
            pl.semaphore_signal(
                known.at[step], inc=1, device_id=peer, device_id_type=MESH
            )
        return len(peers)

    def ring(d):
        return [(c, lax.rem(s + d, ns)), (c, lax.rem(s + ns - d, ns))]

    n0 = tell(0, near)

    def columns(k):
        return slice((k - 1) * LANES, k * LANES)

    def fill_grid(src, dst, rows, real=None):
        def body(k):
            value = src[:, columns(k)]
            if real is not None:
                value = jnp.where(real, value, jnp.zeros_like(value))

            def store():
                dst[k, rows, :] = value

            return store

        each_block(body)

    def fill_cond(j, flow_src, force_src, wet_src, rows, real=None):
        at0 = j * STATES

        def body(k):
            at = columns(k)

            def get(value):
                if real is None:
                    return value
                return jnp.where(real, value, jnp.zeros_like(value))

            d = dep[k, rows, :]
            e = get(flow_src[0, :, at])
            u = get(flow_src[1, :, at])
            v = get(flow_src[2, :, at])
            m = get(wet_src[:, at]).astype(F32) * (0.5 * TIME_STEP)
            force_a = 2.0 * m * get(force_src[0, :, at])
            force_b = 2.0 * m * get(force_src[1, :, at])

            def store():
                eta[at0, k, rows, :] = e
                vel_a[at0, k, rows, :] = u
                vel_b[at0, k, rows, :] = v
                dva[at0, k, rows, :] = d * u
                dvb[at0, k, rows, :] = d * v
                mask[j, k, rows, :] = m
                fa[j, k, rows, :] = force_a
                fb[j, k, rows, :] = force_b

            return store

        each_block(body, GROUP // 2)

    own = pl.ds(HALO, ROWS)
    l_depth.wait()
    fill_grid(grid_own.at[0], dep, own)

    def advance(j, t, k, start, n):
        at = j * STATES + t
        first_lane, last_lane = wide(lane, n) == 0, wide(lane, n) == LANES - 1
        rows, up, dn = (pl.ds(start + d, 8 * n) for d in (0, -1, 1))

        def across(ref):
            here = ref[at, k, rows, :]
            right = jnp.where(first_lane, ref[at, k + 1, rows, :], here)
            left = jnp.where(last_lane, ref[at, k - 1, rows, :], here)
            return here, pltpu.roll(right, LANES - 1, 1) - pltpu.roll(left, 1, 1)

        e, e_across = across(eta)
        _, h_across = across(dvb)
        m = mask[j, k, rows, :]
        keep = 1.0 - (2.0 * FRICTION) * m
        e_next = e - m * (dva[at, k, dn, :] - dva[at, k, up, :] + h_across)
        slope = GRAVITY * m
        u_next = keep * vel_a[at, k, rows, :] + fa[j, k, rows, :]
        u_next = u_next - slope * (eta[at, k, dn, :] - eta[at, k, up, :])
        v_next = keep * vel_b[at, k, rows, :] + fb[j, k, rows, :] - slope * e_across
        return e_next, u_next, v_next

    def put(j, t, k, start, n, state):
        at = j * STATES + t
        rows = pl.ds(start, 8 * n)
        e, u, v = state
        d = dep[k, rows, :]
        eta[at, k, rows, :] = e
        vel_a[at, k, rows, :] = u
        vel_b[at, k, rows, :] = v
        dva[at, k, rows, :] = d * u
        dvb[at, k, rows, :] = d * v

    def first(j, t, start, n):
        def body(k):
            state = advance(j, t - 1, k, start, n)
            return lambda: put(j, t, k, start, n, state)

        each_block(body, GROUP // n)

    def second(j, t, start, n, weight, valid=None):
        def body(k):
            at = j * STATES + t - 2
            rows = pl.ds(start, 8 * n)
            e, u, v = advance(j, t - 1, k, start, n)
            e = 0.5 * (eta[at, k, rows, :] + e)
            u = 0.5 * (vel_a[at, k, rows, :] + u)
            v = 0.5 * (vel_b[at, k, rows, :] + v)
            energy = u * u + v * v
            factor = weight * (TRANSPORT_BASE + energy)
            factor = factor / (1.0 + lim[k, rows, :] * energy)
            add_a, add_b = u * factor, v * factor
            if valid is not None:
                add_a = jnp.where(valid, add_a, 0.0)
                add_b = jnp.where(valid, add_b, 0.0)
            sum_a = qa[k, rows, :] + add_a
            sum_b = qb[k, rows, :] + add_b

            def store():
                put(j, t, k, start, n, (e, u, v))
                qa[k, rows, :] = sum_a
                qb[k, rows, :] = sum_b

            return store

        each_block(body, GROUP // n)

    def interior(j, weight):
        def pair(p, carry, n):
            t = 2 * p + 1
            first(j, t, HALO + t, n)
            place = jnp.concatenate([sub + 8 * i for i in range(n)], 0)
            second(j, t + 1, HALO + t + 1, n, weight, place < ROWS - 2 * (t + 1))
            return carry

        lax.fori_loop(0, 2, functools.partial(pair, n=2), 0)
        for p in range(2, STEPS - 1):
            pair(p, 0, 1)
        first(j, HALF_STEPS - 1, HALO + HALF_STEPS - 1, 1)

    def side_steps(j, side, weight):
        def pair(p, carry):
            t = 2 * p + 1
            first(j, t, jnp.where(side == 0, t, 24 - t), 1)
            t = 2 * p + 2
            second(j, t, jnp.where(side == 0, t, 24 - t), 1, weight)
            return carry

        lax.fori_loop(0, STEPS, pair, 0)
        rows = pl.ds(pl.multiple_of(8 * side, 8), 8)
        held = pl.ds(pl.multiple_of(8 + 8 * side, 8), 8)
        for k in range(1, blocks + 1):
            state = eta[j * STATES + HALF_STEPS, k, held, :]
            surface_twice[j, rows, columns(k)] = 2.0 * state

    l_w.wait()
    w_sum = w_own[0, 0]
    for i in range(1, nc * conds):
        w_sum = w_sum + w_own[0, i]
    w_sum = w_sum.astype(F32)

    def lim_rows():
        l_lim.wait()

        def body(k):
            value = lim_own[:, columns(k)].astype(F32)

            def store():
                lim[k, own, :] = value
                lim[k, 0:8, :] = jnp.zeros((8, LANES), F32)
                lim[k, 24:32, :] = jnp.zeros((8, LANES), F32)

            return store

        each_block(body)

    lim_rows()
    def weight_of(j):
        return w_own[0, conds * c + j].astype(F32)

    def start_cond(j, carry):
        for copy in loads_cond(j):
            copy.wait()
        fill_cond(j, flow_own.at[j], force_own.at[j], wet_own.at[j], own)
        interior(j, weight_of(j))
        return carry

    lax.fori_loop(0, conds, start_cond, 0)
    pl.semaphore_wait(known.at[0], n0)
    n1 = tell(1, near + ring(2))
    l_diff.wait()
    l_bed.wait()
    fill_grid(grid_own.at[1], diff, own)

    def rim_rows(side):
        return pl.ds(pl.multiple_of(24 * side, 8), 8)

    def side_grid(side):
        fill_grid(grid_rim.at[side, 0], dep, rim_rows(side), has(side))

    def side_cond(side, j):
        fill_cond(
            j,
            flow_rim.at[side, j],
            force_rim.at[side, j],
            wet_rim.at[side, j],
            rim_rows(side),
            has(side),
        )
        side_steps(j, side, weight_of(j))

    right_part = lane < LANES // 2

    def beside(left, right):
        return jnp.where(wide(right_part, left.shape[0] // 8), right, left)

    def remote(src, dst, send, recv, peer):
        copy = pltpu.make_async_remote_copy(
            src, dst, send, recv, device_id=peer, device_id_type=MESH
        )
        copy.start()

    def arrive(ref, sem):
        pltpu.make_async_copy(ref, ref, sem).wait()

    scale = (-0.5 * MORPH_FACTOR) / w_sum

    def divergence(start, count, clear):
        n = -(-count // 8)
        rows, up, dn = (pl.ds(7 + start + d, 8 * n) for d in (0, -1, 1))
        held = slice(start, start + count)
        first_lane, last_lane = wide(lane, n) == 0, wide(lane, n) == LANES - 1
        for k in range(1, blocks + 1):
            for ref in (qa, qb):
                ref[k, 24 * clear : 24 * clear + 8, :] = jnp.zeros((8, LANES), F32)

        def body(k):
            here = qb[k, rows, :]
            right = jnp.where(first_lane, qb[k + 1, rows, :], here)
            left = jnp.where(last_lane, qb[k - 1, rows, :], here)
            total = pltpu.roll(right, LANES - 1, 1) - pltpu.roll(left, 1, 1)
            total = scale * (total + (qa[k, dn, :] - qa[k, up, :]))

            def store():
                outbox[(k - 1) // share, (k - 1) % share, held] = total[0:count]

            return store

        each_block(body)
        nothing = jnp.zeros((count, LANES), F32)
        is_right = lax.broadcasted_iota(jnp.int32, (count, LANES), 1) < LANES // 2
        for to in range(nc):
            left = outbox[to - 1, share - 1, held] if to > 0 else nothing
            right = outbox[to + 1, 0, held] if to < nc - 1 else nothing
            outbox[to, share, held] = jnp.where(is_right, right, left)

    def send_edges(side):
        rows = slice(0, 3) if side == 0 else slice(EDGE - 3, EDGE)
        land, recv = (in_dn, dn_recv) if side == 0 else (in_up, up_recv)
        for d in range(nc):
            peer = lax.rem(c + d, nc)
            remote(
                outbox.at[peer, :, rows],
                land.at[d, :, 0:3],
                rs_send.at[1 + side],
                recv,
                (peer, s - 1 + 2 * side),
            )

    def send_rows(start, count):
        held = slice(start, start + count)
        for d in range(1, nc):
            peer = lax.rem(c + d, nc)
            remote(
                outbox.at[peer, :, held],
                inbox.at[d, :, held],
                rs_send.at[0],
                rs_recv,
                (peer, s),
            )

    def early_part(side):
        start = 10 if side == 0 else 0
        divergence(start, 8, 1 - side)
        send_edges(1 - side)
        send_rows(start, 8)

    def late_part(side):
        start = 0 if side == 0 else 8
        divergence(start, 10, side)
        pl.when(has(side))(lambda: send_edges(side))
        send_rows(start, 10)

    def by_slow(part):
        for value in (0, 1):
            pl.when(slow == value)(functools.partial(part, value))

    def before_side(side):
        wait_grid(side, 0)
        side_grid(side)

    def after_first_side():
        pl.semaphore_wait(known.at[1], n1)
        tell(2, near + ring(4))

    first_lane3 = wide(lane, 3) == 0
    last_lane3 = wide(lane, 3) == LANES - 1

    n2, n3 = len(near) + 2, 2

    def between():
        pl.semaphore_wait(known.at[2], n2)
        tell(3, ring(8))
        by_slow(early_part)

    def coefficients():
        wait_grid(fast, 1, 2)
        fill_grid(grid_rim.at[fast, 1], diff, rim_rows(fast))
        wait_grid(slow, 1, 2)
        fill_grid(grid_rim.at[slow, 1], diff, rim_rows(slow), has(slow))

        def faces(k):
            rows, dn = pl.ds(7, 24), pl.ds(8, 24)

            def face(p, q):
                total = p + q
                return SLOPE_COEFF * p * q / jnp.where(total > 0.0, total, 1.0)

            d = diff[k, rows, :]
            right = jnp.where(first_lane3, diff[k + 1, rows, :], d)
            left = jnp.where(last_lane3, diff[k - 1, rows, :], d)
            f_dn = face(d, diff[k, dn, :])
            f_right = face(d, pltpu.roll(right, LANES - 1, 1))
            f_left = face(d, pltpu.roll(left, 1, 1))

            def store():
                kd[k, rows, :] = f_dn
                kr[k, rows, :] = f_right
                kl[k, rows, :] = f_left

            return store

        each_block(faces, GROUP // 4)
        def bed_block(k):
            at = pl.ds(pl.multiple_of(k * LANES, LANES), LANES)
            return (
                grid_rim[0, 2, :, at],
                grid_own[2, :, at],
                grid_rim[1, 2, :, at],
            )

        before = lax.max(share * c - 1, 0)
        after = lax.min(share * (c + 1), blocks - 1)
        beds = [bed_block(share * c + r) for r in range(share)]
        beds.append(tuple(map(beside, bed_block(before), bed_block(after))))
        for r, (above, own_rows, below) in enumerate(beds):
            slice_b[r, 0:8] = jnp.where(s > 0, above, 0.0)
            slice_b[r, 8:24] = own_rows
            slice_b[r, 24:32] = jnp.where(s < ns - 1, below, 0.0)
        for src, dst in ((kd, slice_kd), (kr, slice_kr), (kl, slice_kl)):
            for r in range(share):
                dst[r] = src[share * c + 1 + r]
            dst[share] = beside(src[share * c], src[share * (c + 1) + 1])

    def side_part(i, carry):
        j, on_slow = lax.rem(i, conds), i >= conds
        side = jnp.where(on_slow, slow, fast)
        pl.when(j == 0)(lambda: before_side(side))
        wait_cond(side, j)
        side_cond(side, j)
        pl.when(i == conds - 1)(after_first_side)
        pl.when(i == 2 * conds - 2)(between)
        return carry

    lax.fori_loop(0, 2 * conds, side_part, 0)

    pl.semaphore_wait(known.at[3], n3)
    by_slow(late_part)
    coefficients()
    landed = inbox.at[1:nc, :, 0:EDGE]
    edge_up, edge_dn = in_up.at[:, :, 0:3], in_dn.at[:, :, 0:3]
    arrive(landed, rs_recv)
    total = [outbox[c, :, 0:16], outbox[c, :, 16:EDGE]]
    for d in range(1, nc):
        total[0] = total[0] + inbox[d, :, 0:16]
        total[1] = total[1] + inbox[d, :, 16:EDGE]
    slice_b[:, 7:23] = slice_b[:, 7:23] + total[0]
    slice_b[:, 23:25] = slice_b[:, 23:25] + total[1]
    pl.when(s > 0)(lambda: arrive(edge_up, up_recv))
    pl.when(s < ns - 1)(lambda: arrive(edge_dn, dn_recv))
    for land, start in ((in_up, 6), (in_dn, 23)):
        extra = land[0, :, 0:3]
        for d in range(1, nc):
            extra = extra + land[d, :, 0:3]
        slice_b[:, start : start + 3] = slice_b[:, start : start + 3] + extra

    def image_of(get, face_dn, face_right, face_left, left, right, n):
        rows, up, dn = (slice(8 + d, 8 + d + 8 * n) for d in (0, -1, 1))
        first_lane, last_lane = wide(lane, n) == 0, wide(lane, n) == LANES - 1
        here = get(rows)
        to_right = jnp.where(first_lane, right(rows), here)
        to_left = jnp.where(last_lane, left(rows), here)
        to_dn, to_up = here - get(dn), here - get(up)
        to_right = here - pltpu.roll(to_right, LANES - 1, 1)
        to_left = here - pltpu.roll(to_left, 1, 1)
        f_dn, f_right = face_dn(rows) * to_dn, face_right(rows) * to_right
        image = f_dn + face_dn(up) * to_up + f_right + face_left(rows) * to_left
        return here, image, f_dn * to_dn + f_right * to_right

    def fold(value):
        return value[0:8] + value[8:16]

    def rows_of(ref, k):
        return lambda rows: ref[k, rows, :]

    zero = jnp.zeros((8, LANES), F32)
    bb, bl, ll, lyl = zero, zero, zero, zero
    images = []
    for r in range(share + 1):
        here, image, energy = image_of(
            rows_of(slice_b, r),
            rows_of(slice_kd, r),
            rows_of(slice_kr, r),
            rows_of(slice_kl, r),
            rows_of(slice_b, r - 1 if r else share),
            rows_of(slice_b, min(r + 1, share)),
            3,
        )
        images.append(image)
        if r < share:
            bb, bl, ll = bb + fold(here * here), bl + fold(energy), ll + fold(image * image)
    for r in range(share):
        slice_y[r] = images[r]
        here = images[r][0:16]
        right = jnp.where(wide(lane, 2) == 0, images[r + 1][0:16], here)
        to_right = here - pltpu.roll(right, LANES - 1, 1)
        to_dn = here - slice_y[r, 1:17]
        f_dn, f_right = slice_kd[r, own] * to_dn, slice_kr[r, own] * to_right
        lyl = lyl + fold(f_dn * to_dn + f_right * to_right)
    tile = zero
    for i, value in enumerate((bb, bl, ll, lyl)):
        tile = jnp.where(sub == i, jnp.sum(value, 0, keepdims=True), tile)

    half = ns // 2
    sums[0] = tile
    for e in range(2):
        for d in range(nc):
            if d or e:
                peer = (lax.rem(c + d, nc), lax.rem(s + half * e, ns))
                at = nc * e + d
                remote(sums.at[0, 0:4], sums.at[at, 0:4], sum_send.at[0], sum_recv.at[0], peer)
    mine = pl.ds(share * c + 1, share)
    b[mine, 7:23] = slice_b[0:share, 7:23]
    b[mine, 23:25] = slice_b[0:share, 23:25]

    others = sums.at[1 : 2 * nc, 0:4]
    arrive(others, sum_recv.at[0])
    totals[0] = jnp.sum(sums[...], 0)
    base, place = s - lax.rem(s, half), lax.rem(s, half)
    for d in range(1, half):
        peer = (c, base + lax.rem(place + d, half))
        remote(totals.at[0, 0:4], totals.at[d, 0:4], sum_send.at[1], sum_recv.at[1], peer)

    b_own = slice_b.at[0:share, 7:25]
    for d in range(1, nc):
        peer = (lax.rem(c + d, nc), s)
        remote(b_own, b.at[mine, 7:25], ag_send, ag_recv, peer)

    gathered = b.at[1 : blocks + 1 - share, 7:25]
    arrive(gathered, ag_recv)

    def strip(k):
        _, image, _ = image_of(
            rows_of(b, k),
            rows_of(kd, k),
            rows_of(kr, k),
            rows_of(kl, k),
            rows_of(b, k - 1),
            rows_of(b, k + 1),
            2,
        )

        def store():
            y[k, 0:16] = image

        return store

    each_block(strip, GROUP // 2)
    halves = totals.at[1:half, 0:4]
    for side in (0, 1):

        def sent(side=side):
            of_grid, of_cond = rim_copies(side, 1 - side)
            for at in range(3):
                of_grid(at).wait_send()
            for j in range(conds):
                for copy in of_cond(j):
                    copy.wait_send()
            arrive(edge_up, rs_send.at[1 + side])

        pl.when(has(side))(sent)
    arrive(landed, rs_send.at[0])
    arrive(gathered, ag_send)
    arrive(others, sum_send.at[0])
    arrive(halves, sum_send.at[1])

    arrive(halves, sum_recv.at[1])
    total = jnp.sum(jnp.sum(totals[...], 0), 1, keepdims=True)
    s_bb, s_bl, s_ll, s_lyl = (total[i : i + 1] for i in range(4))
    m1, m2, m3 = s_bl / s_bb, s_ll / s_bb, s_lyl / s_bb
    alpha0 = 1.0 / (1.0 + m1)
    beta = (m2 - m1 * m1) * alpha0 * alpha0
    p_b = m1 * alpha0 + beta
    p_l = alpha0
    pp = p_b * p_b - 2.0 * p_b * p_l * m1 + p_l * p_l * m2
    plp = p_b * p_b * m1 - 2.0 * p_b * p_l * m2 + p_l * p_l * m3
    alpha1 = beta / (pp + plp)
    x_b = alpha0 + alpha1 * p_b
    x_l = -alpha1 * p_l

    x_b, x_l = 2.0 * x_b, 2.0 * x_l
    for k in range(1, blocks + 1):
        bed_twice[:, columns(k)] = x_b * b[k, own] + x_l * y[k, 0:16]


def local(nc, ns, flow, forcing, wet, depth, limiter, weights, bed, diffusivity):
    conds, ny = flow.shape[0], flow.shape[-1]
    blocks = ny // LANES
    dma = pltpu.SemaphoreType.DMA

    def vmem(*shape, dtype=F32):
        return pltpu.VMEM(shape, dtype)

    def state():
        return vmem(conds * STATES, blocks + 2, TALL, LANES)

    def per_cond():
        return vmem(conds, blocks + 2, TALL, LANES)

    def grid():
        return vmem(blocks + 2, TALL, LANES)

    share = blocks // nc
    rims = 3 + 5 * conds
    any_space = pl.BlockSpec(memory_space=pl.ANY)
    in_vmem = pl.BlockSpec(memory_space=pltpu.VMEM)
    surface_twice, bed_twice = pl.pallas_call(
        functools.partial(kernel, nc, ns),
        out_shape=(
            pltpu.VMEM((conds, ROWS, ny), F32),
            pltpu.VMEM((ROWS, ny), F32),
        ),
        in_specs=[any_space] * 8,
        out_specs=(in_vmem, in_vmem),
        scratch_shapes=[
            vmem(conds, 3, ROWS, ny),
            vmem(conds, 2, ROWS, ny),
            vmem(conds, ROWS, ny, dtype=jnp.int32),
            vmem(3, ROWS, ny),
            vmem(ROWS, ny, dtype=jnp.int32),
            pltpu.SMEM((1, nc * conds), jnp.int32),
            vmem(2, conds, 3, HALO, ny),
            vmem(2, conds, 2, HALO, ny),
            vmem(2, conds, HALO, ny, dtype=jnp.int32),
            vmem(2, 3, HALO, ny),
            state(),
            state(),
            state(),
            state(),
            state(),
            per_cond(),
            per_cond(),
            per_cond(),
            grid(),
            grid(),
            grid(),
            grid(),
            vmem(nc, share + 1, 24, LANES),
            vmem(nc, share + 1, 24, LANES),
            vmem(nc, share + 1, 8, LANES),
            vmem(nc, share + 1, 8, LANES),
            grid(),
            grid(),
            grid(),
            grid(),
            grid(),
            vmem(blocks + 1, ROWS, LANES),
            vmem(share + 1, TALL + 8, LANES),
            vmem(share, 24, LANES),
            vmem(share + 1, TALL, LANES),
            vmem(share + 1, TALL, LANES),
            vmem(share + 1, TALL, LANES),
            vmem(2 * nc, 8, LANES),
            vmem(ns // 2, 8, LANES),
            dma((5 + 3 * conds,)),
            dma((2, rims)),
            dma((2, rims)),
            dma((3,)),
            dma(()),
            dma(()),
            dma(()),
            dma(()),
            dma(()),
            dma((2,)),
            dma((2,)),
            pltpu.SemaphoreType.REGULAR((4,)),
        ],
        compiler_params=pltpu.CompilerParams(
            collective_id=0, has_side_effects=True, vmem_limit_bytes=58 << 20
        ),
        cost_estimate=pl.CostEstimate(
            flops=20_000_000, bytes_accessed=4_000_000, transcendentals=0
        ),
        name="morphology",
    )(flow, forcing, wet, depth, limiter, weights.reshape(1, -1), bed, diffusivity)
    return 0.5 * surface_twice, 0.5 * bed_twice


def solution(mesh):
    in_specs = (
        P("cond", None, "space", None),
        P("cond", None, "space", None),
        P("cond", "space", None),
        P("space", None),
        P("space", None),
        P(),
        P("space", None),
        P("space", None),
    )
    out_specs = (P("cond", "space", None), P("space", None))
    body = functools.partial(local, mesh.shape["cond"], mesh.shape["space"])
    return jax.shard_map(body, mesh=mesh, in_specs=in_specs, out_specs=out_specs, check_vma=False)
```
